256 devices in a mesh: dp: 64 (over y, z, core), node: 4 (over x).
Axes of the slice: x: 4, y: 4, z: 8, core: 2. Of those that a mesh axis runs over, the one named last changes fastest.
Arguments:
- hidden: bfloat16 [131072, 256], P(('dp', 'node')), may hold values from -6 to 6
- out_grad: bfloat16 [131072, 5120], P(('dp', 'node')), may hold values from -0.3125 to 0.3125
- momentum: float32 [64, 256, 5120], P('dp', 'node')
- positions: int32 [64, 4, 80, 32], P(None, 'node'), may hold values from 0 to 4095, as said below
- weights: float32 [256, 5120], P('node'), may hold values from -6 to 6
Outputs:
- new_momentum: float32 [64, 256, 5120], P('dp', 'node')
- update: float32 [256, 5120], P('node')
- gathered: bfloat16 [256, 5120], replicated
The draws below stay inside these ranges and needn't reach their ends.
Inputs may be any that keep to these rules, and one draw needn't show every extreme that they name: Within each group the 32 positions are distinct; position number j lies in the j-th of 32 equal consecutive ranges of the 4096 positions.
All inputs are finite; a program needn't handle non-finite values.
Results may differ from the reference program's by a relative error of at most 0.0039.
Values may be sent and summed in bfloat16 or wider, within the bound.
No kernel may reach another device: no remote copies, remote signals or barrier semaphores. Data moves between devices by JAX's collectives and lax.ppermute only.
A program may use at most 64 MiB of HBM per device.

```python
import jax
import jax.numpy as jnp
from jax import lax

D = 5120
CH = 64
K = 32
TOK_DEV = 512
ROWS = 256
NB = 80
TOKENS = 131072
N_DP = 64
N_NODE = 4


def draw_momentum(key, part):
    key = jax.random.fold_in(key, 11)
    first, second, third = jax.random.split(key, 3)
    row_scale = jnp.exp(jax.random.uniform(first, (N_DP, ROWS, 1), minval=0.0, maxval=1.15))
    col_scale = jnp.exp(jax.random.uniform(second, (1, 1, D), minval=0.0, maxval=1.15))
    base = jax.random.normal(third, (N_DP, ROWS, D))
    return (base * row_scale * col_scale).astype(jnp.float32)


def draw_positions(key, part):
    key = jax.random.fold_in(key, 23)
    span = CH * CH // K
    offsets = jax.random.randint(key, (N_DP, N_NODE, D // CH, K), 0, span)
    chosen = offsets + span * jnp.arange(K, dtype=jnp.int32)
    chosen = chosen.at[0, 0, 0, 0].set(0).at[0, 0, 0, K - 1].set(CH * CH - 1)
    return chosen.astype(jnp.int32)


def level_of(key, dims, cuts, smallest, top_value):
    def one(axis_at, shards_of):
        steps = jax.random.uniform(jax.random.fold_in(jax.random.fold_in(key, 6), axis_at), (shards_of,), jnp.float32, smallest / len(cuts), top_value / len(cuts))
        return jnp.repeat(jnp.exp(steps), dims[axis_at] // shards_of).reshape((-1,) + (1,) * (len(dims) - axis_at - 1))

    level = one(*cuts[0])
    for cut in cuts[1:]:
        level = level * one(*cut)
    return level


def normal_values(key, shape, spread, most, pieces=(), kind=jnp.bfloat16):
    values = spread * jax.random.normal(key, shape, jnp.float32)
    if pieces:
        values = values * level_of(key, shape, pieces, -0.22, 0.18)
    return jnp.clip(values, -most, most).astype(kind)


def setup_inputs(seed: int = 0) -> dict:
    key_list = jax.random.split(jax.random.key(seed), 6)
    hidden = normal_values(key_list[0], (TOKENS, ROWS), 1.0, 6.0, ((0, 256),))
    out_grad = normal_values(key_list[1], (TOKENS, D), ((TOK_DEV * N_NODE) ** -0.5), 0.3125, ((0, 256),))
    momentum = draw_momentum(jax.random.fold_in(key_list[5], 71), 0)
    positions = draw_positions(jax.random.fold_in(key_list[5], 71), 0)
    weights = normal_values(key_list[4], (ROWS, D), 1.0, 6.0, ((0, 4),), jnp.float32)
    return dict(hidden=hidden, out_grad=out_grad, momentum=momentum, positions=positions, weights=weights)


def basis(size):
    freq = jnp.arange(size, dtype=jnp.float32)[:, None]
    place = jnp.arange(size, dtype=jnp.float32)[None, :]
    table = jnp.cos(jnp.pi * (2.0 * place + 1.0) * freq / (2.0 * size)) * jnp.sqrt(2.0 / size)
    return jnp.where(freq == 0, table * jnp.sqrt(0.5), table)

def forward(matrix, table):
    blocks = matrix.reshape(ROWS // CH, CH, NB, CH)
    return jnp.einsum('in,anbl,kl->aibk', table, blocks, table, precision=lax.Precision.HIGHEST)

def inverse(coeffs, table):
    full = jnp.einsum('in,aibk,kl->anbl', table, coeffs, table, precision=lax.Precision.HIGHEST)
    return full.reshape(ROWS, D)

def reference(hidden, out_grad, momentum, positions, weights):
    table = basis(CH)
    per_rep = TOK_DEV * N_NODE
    row_ids = jnp.arange(ROWS // CH)[:, None, None]
    col_ids = jnp.arange(NB)[None, :, None]

    def one_replica(total, index):
        start = (index * per_rep).astype(jnp.int32)
        acts = lax.dynamic_slice_in_dim(hidden, start, per_rep, 0)
        grads = lax.dynamic_slice_in_dim(out_grad, start, per_rep, 0)
        grad = lax.dot_general(acts, grads, (((0,), (0,)), ((), ())), preferred_element_type=jnp.float32)
        moment = 0.9 * momentum[index] + grad
        coeffs = forward(moment, table)
        flat = coeffs.transpose(0, 2, 1, 3).reshape(ROWS // CH, NB, CH * CH)
        chosen = positions[index]
        values = jnp.take_along_axis(flat, chosen, axis=2)
        sparse = jnp.zeros_like(flat).at[row_ids, col_ids, chosen].set(values)
        sparse = sparse.reshape(ROWS // CH, NB, CH, CH).transpose(0, 2, 1, 3)
        new_moment = moment - inverse(sparse, table)
        return (total + sparse, new_moment)
    start_total = jnp.zeros((ROWS // CH, CH, NB, CH), jnp.float32)
    total, new_momentum = lax.scan(one_replica, start_total, jnp.arange(N_DP, dtype=jnp.int32))
    merged = jnp.einsum('in,aibk,kl->anbl', table, total, table, precision=lax.Precision.HIGHEST)
    scale = jnp.sqrt(lax.optimization_barrier(jnp.mean(merged * merged, axis=(1, 3), keepdims=True)) + 1e-06)
    update = jnp.tanh(merged / scale).reshape(ROWS, D)
    gathered = (weights - 0.05 * update).astype(jnp.bfloat16)
    return (new_momentum, update, gathered)
```

```python
import functools

import jax
import jax.numpy as jnp
import ml_dtypes
import numpy as np
from jax import lax
from jax.experimental import pallas as pl
from jax.experimental.pallas import tpu as pltpu
from jax.sharding import PartitionSpec as P

F32 = jnp.float32
BF16 = jnp.bfloat16
VMEM_LIMIT = 48 * 1024 * 1024


def split_np(x):
    hi = x.astype(ml_dtypes.bfloat16)
    lo = (x - hi.astype(np.float64)).astype(ml_dtypes.bfloat16)
    return hi, lo


def padded(count):
    return -(-count // 16) * 16


def basis(size):
    freq = np.arange(size, dtype=np.float64)[:, None]
    place = np.arange(size, dtype=np.float64)[None, :]
    table = np.cos(np.pi * (2.0 * place + 1.0) * freq / (2.0 * size)) * np.sqrt(2.0 / size)
    return np.where(freq == 0, table * np.sqrt(0.5), table)


def constants(blocks):
    table = basis(64)
    order = np.concatenate([np.arange(0, 64, 2), np.arange(1, 64, 2)])
    rows = table[order]
    hi, lo = split_np(rows)
    tiled = np.concatenate([np.tile(hi, (4, 4)), np.tile(lo, (4, 4))]).astype(np.float32)
    forward = np.concatenate([hi, hi, lo], axis=1)
    inverse = np.concatenate([hi.T, hi.T, lo.T], axis=1)
    pair = np.kron(np.eye(2), table)
    pair_hi, pair_lo = split_np(pair)
    look = np.concatenate([pair_hi, pair_lo], axis=0)
    spread = np.zeros((2, 2, 64, 2, 2, 64))
    for p in range(2):
        for t in range(2):
            spread[p, t, :, t, p, :] = table
    wide_hi, wide_lo = split_np(spread.reshape(256, 256))
    ones = np.kron(np.eye(2), np.ones((64, 64))).astype(ml_dtypes.bfloat16)
    half = blocks // 2
    expand = np.zeros((padded(half), half * 64), ml_dtypes.bfloat16)
    for b in range(half):
        expand[(b % 2) * (half // 2) + b // 2, b * 64 : (b + 1) * 64] = 1
    return dict(
        tiled=tiled,
        forward=forward,
        inverse=inverse,
        look=look,
        wide_hi=wide_hi,
        wide_lo=wide_lo,
        ones=ones,
        expand=expand,
    )


def split2(x):
    hi = x.astype(BF16)
    return hi, (x - hi.astype(F32)).astype(BF16)


def mm(a, b):
    return jnp.dot(a, b, preferred_element_type=F32)


def mm_nt(a, b):
    return lax.dot_general(a, b, (((1,), (1,)), ((), ())), preferred_element_type=F32)


def packed(x):
    hi, lo = split2(x)
    return jnp.concatenate([hi, lo, hi], axis=0)


def grad_kernel(me_ref, hid_ref, tiled_ref, g_ref, own_ref, r1_ref, r2_ref, r3_ref, hc_ref):
    @pl.when(pl.program_id(0) == 0)
    def _():
        me = me_ref[0]
        row = lax.broadcasted_iota(jnp.int32, (256, 256), 0) >> 6
        col = lax.broadcasted_iota(jnp.int32, (256, 256), 1) >> 6
        keep = ((col - row - me + 8) & 3) == 0
        hi = jnp.where(keep, tiled_ref[0:256, :], 0.0).astype(BF16)
        lo = jnp.where(keep, tiled_ref[256:512, :], 0.0).astype(BF16)
        acts = mm_nt(hi, hid_ref[...]) + mm_nt(lo, hid_ref[...])
        acts_hi, acts_lo = split2(acts)
        hc_ref[0:256, :] = acts_hi
        hc_ref[256:512, :] = acts_lo

    acc = mm(hc_ref[...], g_ref[...])
    own_ref[...] = acc[0:64] + acc[256:320]
    r1_ref[...] = (acc[64:128] + acc[320:384]).astype(BF16)
    r2_ref[...] = (acc[128:192] + acc[384:448]).astype(BF16)
    r3_ref[...] = (acc[192:256] + acc[448:512]).astype(BF16)


def grad_part(me, hidden, tiled, out_grad, part):
    tokens, width = out_grad.shape
    half = width // 2
    block = 640
    steps = half // block
    outs = [jax.ShapeDtypeStruct((64, half), d) for d in (F32, BF16, BF16, BF16)]
    whole = lambda shape: pl.BlockSpec(shape, lambda i: (0, 0))
    return pl.pallas_call(
        grad_kernel,
        grid=(steps,),
        in_specs=[
            pl.BlockSpec(memory_space=pltpu.SMEM),
            whole((tokens, 256)),
            whole((512, 256)),
            pl.BlockSpec((tokens, block), lambda i: (0, i + part * steps)),
        ],
        out_specs=[pl.BlockSpec((64, block), lambda i: (0, i))] * 4,
        out_shape=outs,
        scratch_shapes=[pltpu.VMEM((512, tokens), BF16)],
        compiler_params=pltpu.CompilerParams(vmem_limit_bytes=VMEM_LIMIT),
        name="grad_part",
    )(me, hidden, tiled, out_grad)


def prep_kernel(mom_ref, off_ref, expand_ref, forward_ref, look_ref, row_ref, look_out_ref):
    row_ref[...] = 0.9 * mm(forward_ref[...], packed(mom_ref[...]))
    target = mm(off_ref[...], expand_ref[...])
    width = target.shape[1]
    lane = (lax.broadcasted_iota(jnp.int32, target.shape, 1) & 63).astype(F32)
    first = jnp.where(target == lane, 1.0, 0.0)
    second = jnp.where(target == lane + 64.0, 1.0, 0.0)
    mask = jnp.concatenate([first, second], axis=0).astype(BF16)
    for t in range(width // 128):
        piece = mask[:, t * 128 : (t + 1) * 128]
        look_out_ref[:, t * 128 : (t + 1) * 128] = mm(
            jnp.concatenate([piece, piece], axis=1), look_ref[...]
        )


def prep(momentum, off, consts):
    width = momentum.shape[1]
    block = 1280
    per = width // (2 * block)
    count = off.shape[2]
    whole = lambda x: pl.BlockSpec(x.shape, lambda i: (0, 0))
    cols = lambda rows: pl.BlockSpec((rows, block), lambda i: (0, i))
    return pl.pallas_call(
        prep_kernel,
        grid=(width // block,),
        in_specs=[
            cols(64),
            pl.BlockSpec((None, 32, count), lambda i: (i // per, 0, 0)),
            pl.BlockSpec((count, block), lambda i: (0, i % per)),
            whole(consts["forward"]),
            whole(consts["look"]),
        ],
        out_specs=[cols(64), cols(64)],
        out_shape=[jax.ShapeDtypeStruct((64, width), F32)] * 2,
        compiler_params=pltpu.CompilerParams(vmem_limit_bytes=VMEM_LIMIT),
        name="prep",
    )(momentum, off, consts["expand"], consts["forward"], consts["look"])


def values_kernel(
    own_ref, near_ref, far_ref, row_ref, look_ref, expand_ref, sum_ref, vals_ref, turned_ref
):
    total = (
        own_ref[...] + near_ref[...].astype(F32) + far_ref[...].astype(F32) + row_ref[...]
    )
    sum_ref[...] = total
    prod = total * look_ref[...]
    prod = prod[0:32] + prod[32:64]
    hi, rest = split2(prod)
    mid, low = split2(prod - hi.astype(F32))
    expand = expand_ref[...]
    vals_ref[...] = mm_nt(expand, hi) + mm_nt(expand, mid) + mm_nt(expand, low)
    turned_ref[...] = mm_nt(hi, expand) + mm_nt(mid, expand) + mm_nt(low, expand)


def values_part(own, near, far, row, look, consts, part):
    half = own.shape[1]
    count = consts["expand"].shape[0]
    whole = lambda shape: pl.BlockSpec(shape, lambda i: (0, 0))
    cols = lambda rows: pl.BlockSpec((rows, half), lambda i: (0, part))
    return pl.pallas_call(
        values_kernel,
        grid=(1,),
        in_specs=[whole((64, half))] * 3 + [cols(64), cols(64)]
        + [whole((count, half))],
        out_specs=[whole((64, half)), whole((count, 32)), whole((32, count))],
        out_shape=[
            jax.ShapeDtypeStruct((64, half), F32),
            jax.ShapeDtypeStruct((count, 32), F32),
            jax.ShapeDtypeStruct((32, count), F32),
        ],
        compiler_params=pltpu.CompilerParams(vmem_limit_bytes=VMEM_LIMIT),
        name="values_part",
    )(own, near, far, row, look, consts["expand"])


def total_kernel(
    off_ref, val_ref, w_ref, hi_ref, lo_ref, inverse_ref, ones_ref,
    update_ref, s0_ref, s1_ref, t_ref, z_ref,
):
    sources, tiles, _ = off_ref.shape
    index = lax.broadcasted_iota(jnp.int32, (128, 128), 0)

    def one_tile(m, carry):
        acc = jnp.zeros((128, 128), F32)
        for r in range(sources):
            place = off_ref[r, pl.ds(m, 1), :]
            value = val_ref[r, pl.ds(m, 1), :]
            acc = acc + jnp.where(index == place, value, 0.0)
        t_ref[m] = acc
        return carry

    lax.fori_loop(0, tiles, one_tile, 0)
    pairs = tiles // 2
    for q in range(pairs):
        both = jnp.concatenate([t_ref[q].T, t_ref[pairs + q].T], axis=1)
        hi, lo = split2(both)
        mixed = mm(hi, hi_ref[...]) + mm(lo, hi_ref[...]) + mm(hi, lo_ref[...])
        for x in range(4):
            lanes = slice((4 * q + x) * 128, (4 * q + x + 1) * 128)
            z_ref[0:32, lanes] = mixed[x * 32 : (x + 1) * 32, 0:128]
            z_ref[32:64, lanes] = mixed[x * 32 : (x + 1) * 32, 128:256]
    merged = mm(inverse_ref[...], packed(z_ref[...]))
    width = merged.shape[1]
    count = width // 128
    square = merged * merged
    part = square[0:8]
    for i in range(1, 8):
        part = part + square[i * 8 : (i + 1) * 8]
    part = jnp.concatenate([part[:, t * 128 : (t + 1) * 128] for t in range(count)], axis=0)
    hi, rest = split2(part)
    mid, low = split2(part - hi.astype(F32))
    ones = ones_ref[...]
    summed = mm(hi, ones) + mm(mid, ones) + mm(low, ones)
    for t in range(count):
        lanes = slice(t * 128, (t + 1) * 128)
        mean = jnp.sum(summed[t * 8 : (t + 1) * 8], axis=0, keepdims=True) * (1.0 / 4096.0)
        update = jnp.tanh(merged[:, lanes] * lax.rsqrt(mean + 1e-06))
        update_ref[:, lanes] = update
        stepped = (w_ref[:, lanes] - 0.05 * update).astype(BF16)
        if t < count // 2:
            s0_ref[:, lanes] = stepped
        else:
            s1_ref[:, slice((t - count // 2) * 128, (t - count // 2 + 1) * 128)] = stepped


def total_part(off, vals, weights, consts):
    half = weights.shape[1]
    return pl.pallas_call(
        total_kernel,
        out_shape=[
            jax.ShapeDtypeStruct((64, half), F32),
            jax.ShapeDtypeStruct((64, half // 2), BF16),
            jax.ShapeDtypeStruct((64, half // 2), BF16),
        ],
        scratch_shapes=[
            pltpu.VMEM((off.shape[1], 128, 128), F32),
            pltpu.VMEM((64, half), F32),
        ],
        compiler_params=pltpu.CompilerParams(vmem_limit_bytes=VMEM_LIMIT),
        name="total_part",
    )(
        off, vals, weights, consts["wide_hi"], consts["wide_lo"], consts["inverse"],
        consts["ones"],
    )


def moment_kernel(sum_ref, look_ref, turned_ref, expand_ref, inverse_ref, out_ref):
    turned = turned_ref[...]
    hi, rest = split2(turned)
    mid, low = split2(turned - hi.astype(F32))
    expand = expand_ref[...]
    spread = mm(hi, expand) + mm(mid, expand) + mm(low, expand)
    left = sum_ref[...] - jnp.concatenate([spread, spread], axis=0) * look_ref[...]
    out_ref[...] = mm(inverse_ref[...], packed(left))


def moment_part(sum_a, sum_b, look, turned_a, turned_b, consts):
    half = sum_a.shape[1]
    width = 2 * half
    count = consts["expand"].shape[0]
    turned = jnp.stack([turned_a, turned_b])
    total = jnp.stack([sum_a, sum_b])
    block = 1280
    per = half // block
    whole = lambda x: pl.BlockSpec(x.shape, lambda i: (0, 0))
    return pl.pallas_call(
        moment_kernel,
        grid=(width // block,),
        in_specs=[
            pl.BlockSpec((None, 64, block), lambda i: (i // per, 0, i % per)),
            pl.BlockSpec((64, block), lambda i: (0, i)),
            pl.BlockSpec((None, 32, count), lambda i: (i // per, 0, 0)),
            pl.BlockSpec((count, block), lambda i: (0, i % per)),
            whole(consts["inverse"]),
        ],
        out_specs=pl.BlockSpec((64, block), lambda i: (0, i)),
        out_shape=jax.ShapeDtypeStruct((64, width), F32),
        compiler_params=pltpu.CompilerParams(vmem_limit_bytes=VMEM_LIMIT),
        name="moment_part",
    )(total, look, turned, consts["expand"], consts["inverse"])


def place_kernel(where_ref, *refs):
    pieces = refs[0:16]
    halves = refs[16:18]
    gathered_ref, update_ref, sem = refs[18:]
    me = where_ref[0]
    core = where_ref[1]
    quarter = pieces[0].shape[1]
    copies = []
    for at, piece in enumerate(pieces):
        side, rest = divmod(at, 8)
        ahead, part = divmod(rest, 2)
        row = pl.multiple_of(((me + ahead) & 3) * 64, 64)
        chosen = core if side == 0 else 1 - core
        col = pl.multiple_of(chosen * (2 * quarter) + part * quarter, 128)
        copies.append(
            pltpu.make_async_copy(
                piece, gathered_ref.at[pl.ds(row, 64), pl.ds(col, quarter)], sem.at[at]
            )
        )
    for side, half in enumerate(halves):
        chosen = core if side == 0 else 1 - core
        col = pl.multiple_of(chosen * (2 * quarter), 128)
        copies.append(
            pltpu.make_async_copy(
                half, update_ref.at[:, pl.ds(col, 2 * quarter)], sem.at[16 + side]
            )
        )
    for copy in copies:
        copy.start()
    for copy in copies:
        copy.wait()


def place(where, pieces, halves):
    quarter = pieces[0].shape[1]
    anywhere = pl.BlockSpec(memory_space=pl.ANY)
    return pl.pallas_call(
        place_kernel,
        in_specs=[pl.BlockSpec(memory_space=pltpu.SMEM)]
        + [pl.BlockSpec(memory_space=pltpu.VMEM)] * 18,
        out_specs=[anywhere, anywhere],
        out_shape=[
            jax.ShapeDtypeStruct((256, 4 * quarter), BF16),
            jax.ShapeDtypeStruct((64, 4 * quarter), F32),
        ],
        scratch_shapes=[pltpu.SemaphoreType.DMA((18,))],
        compiler_params=pltpu.CompilerParams(vmem_limit_bytes=VMEM_LIMIT),
        name="place",
    )(where, *pieces, *halves)


def per_device(n_dp, hidden, out_grad, momentum, positions, weights):
    width = weights.shape[1]
    half = width // 2
    blocks = positions.shape[2]
    kept = positions.shape[3]
    consts = {k: jnp.asarray(v) for k, v in constants(blocks).items()}
    me = lax.axis_index("node").astype(jnp.int32)
    replica = lax.axis_index("dp").astype(jnp.int32)
    core = replica & 1
    ahead = [(i, (i + 1) % 4) for i in range(4)]
    back = [(i, (i + 3) % 4) for i in range(4)]
    sibling = [(i, i ^ 1) for i in range(n_dp)]
    right = lambda x: lax.ppermute(x, "node", ahead)
    left = lambda x: lax.ppermute(x, "node", back)
    swap = lambda x: lax.ppermute(x, "dp", sibling)

    mine = me[None]
    own_a, r1_a, r2_a, r3_a = grad_part(mine, hidden, consts["tiled"], out_grad, 0)
    relay_a = right(r2_a)
    near_a = left(r3_a)
    own_b, r1_b, r2_b, r3_b = grad_part(mine, hidden, consts["tiled"], out_grad, 1)
    relay_b = left(r2_b)
    near_b = right(r1_b)
    far_a = right(relay_a + r1_a)
    far_b = left(relay_b + r3_b)

    offsets = (positions[:, 0] & 127).reshape(n_dp, 2, blocks // 4, 2, kept)
    offsets = offsets.transpose(0, 1, 3, 2, 4).reshape(n_dp, 2, blocks // 2, kept)
    own_off = lax.dynamic_index_in_dim(offsets, replica, 0, keepdims=False)
    own_off = own_off.transpose(0, 2, 1).astype(BF16)
    own_off = jnp.pad(own_off, ((0, 0), (0, 0), (0, padded(blocks // 2) - blocks // 2)))
    half_off = lax.dynamic_index_in_dim(offsets, core, 1, keepdims=False)
    tiles = blocks * kept // 256
    half_off = half_off.reshape(n_dp, tiles, 128)
    half_weights = lax.dynamic_slice_in_dim(weights, core * half, half, axis=1)

    row, look = prep(momentum[0], own_off, consts)
    sum_a, vals_a, turned_a = values_part(own_a, near_a, far_a, row, look, consts, 0)
    sum_b, vals_b, turned_b = values_part(own_b, near_b, far_b, row, look, consts, 1)

    sent = jnp.stack([vals_a, vals_b])[:, : blocks // 2].reshape(2, tiles, 128)
    sent = jnp.broadcast_to(sent[None], (n_dp // 2, 2, tiles, 128)).reshape(n_dp, tiles, 128)
    every = lax.all_to_all(sent, "dp", 0, 0, tiled=True)

    update_half, s0, s1 = total_part(half_off, every, half_weights, consts)
    back0 = right(s0)
    front1 = left(s1)
    back1 = right(s1)
    front0 = left(s0)
    over0 = right(back0)
    over1 = left(front1)
    pieces = [s0, s1, front0, front1, over0, over1, back0, back1]
    update_other = swap(update_half)
    others = [swap(x) for x in pieces]

    sum_a, sum_b, s0 = lax.optimization_barrier((sum_a, sum_b, s0))
    new_moment = moment_part(sum_a, sum_b, look, turned_a, turned_b, consts)
    where = jnp.stack([me, core])
    gathered, update = place(where, pieces + others, [update_half, update_other])
    return (new_moment[None], update, gathered)


def solution(mesh):
    return jax.shard_map(
        functools.partial(per_device, mesh.shape["dp"]),
        mesh=mesh,
        in_specs=(
            P(("dp", "node"), None),
            P(("dp", "node"), None),
            P("dp", "node", None),
            P(None, "node", None, None),
            P("node", None),
        ),
        out_specs=(P("dp", "node", None), P("node", None), P()),
        check_vma=False,
    )
```

```python
import functools

import jax
import jax.numpy as jnp
import ml_dtypes
import numpy as np
from jax import lax
from jax.experimental import pallas as pl
from jax.experimental.pallas import tpu as pltpu
from jax.sharding import Mesh
from jax.sharding import PartitionSpec as P

F32 = jnp.float32
BF16 = jnp.bfloat16
VMEM_LIMIT = 32 * 1024 * 1024


def split_np(x):
    hi = x.astype(ml_dtypes.bfloat16)
    lo = (x - hi.astype(np.float64)).astype(ml_dtypes.bfloat16)
    return hi, lo


def basis(size):
    freq = np.arange(size, dtype=np.float64)[:, None]
    place = np.arange(size, dtype=np.float64)[None, :]
    table = np.cos(np.pi * (2.0 * place + 1.0) * freq / (2.0 * size)) * np.sqrt(2.0 / size)
    return np.where(freq == 0, table * np.sqrt(0.5), table)


def constants(blocks, shares):
    table = basis(64)
    order = np.concatenate([np.arange(0, 64, 2), np.arange(1, 64, 2)])
    hi, lo = split_np(table[order])
    tiled = np.concatenate([np.tile(hi, (4, 4)), np.tile(lo, (4, 4))]).astype(np.float32)
    forward = np.concatenate([hi, hi, lo], axis=1)
    inverse = np.concatenate([hi.T, hi.T, lo.T], axis=1)
    look = np.concatenate(split_np(np.kron(np.eye(2), table)), axis=0)
    spread = np.zeros((2, 64, 2, 2, 2, 64))
    for p in range(2):
        for t in range(2):
            spread[t, :, p, t, p, :] = table
    wide_hi, wide_lo = split_np(spread.reshape(128, 512))
    wide = np.concatenate([wide_hi, wide_hi], axis=0)
    ones = np.kron(np.eye(2), np.ones((64, 64))).astype(ml_dtypes.bfloat16)
    expand = np.kron(np.eye(blocks), np.ones((1, 64))).astype(ml_dtypes.bfloat16)
    per = blocks // shares
    gather = np.zeros((4, shares, 4, blocks * 64), ml_dtypes.bfloat16)
    for b in range(blocks):
        q, x = divmod(b % per, 4)
        gather[x, b // per, q, b * 64 : (b + 1) * 64] = 1
    gather = gather.reshape(16 * shares, blocks * 64)
    return dict(
        tiled=tiled, forward=forward, inverse=inverse, look=look, wide=wide, wide_lo=wide_lo,
        ones=ones, expand=expand, gather=gather,
    )


def split2(x):
    hi = x.astype(BF16)
    return hi, (x - hi.astype(F32)).astype(BF16)


def mm(a, b):
    return jnp.dot(a, b, preferred_element_type=F32)


def mm_nt(a, b):
    return lax.dot_general(a, b, (((1,), (1,)), ((), ())), preferred_element_type=F32)


def packed(x):
    hi, lo = split2(x)
    return jnp.concatenate([hi, lo, hi], axis=0)


def hbm(*arrays):
    return [pltpu.with_memory_space_constraint(x, pltpu.HBM) for x in arrays]


PARAMS = pltpu.CompilerParams(vmem_limit_bytes=VMEM_LIMIT)
STEP = 1280


def whole(shape):
    return pl.BlockSpec(shape, lambda i: (0,) * len(shape))


def columns(rows):
    return pl.BlockSpec((rows, STEP), lambda i: (0, i))


def grad_kernel(
    me_ref, hid_ref, tiled_ref, g_ref, own_ref, r1_ref, r2_ref, r3_ref, hc_ref
):
    step = pl.program_id(0)

    @pl.when(step == 0)
    def _():
        me = me_ref[0]
        row = lax.broadcasted_iota(jnp.int32, (256, 256), 0) >> 6
        col = lax.broadcasted_iota(jnp.int32, (256, 256), 1) >> 6
        keep = ((col - row - me + 8) & 3) == 0
        hi = jnp.where(keep, tiled_ref[0:256, :], 0.0).astype(BF16)
        lo = jnp.where(keep, tiled_ref[256:512, :], 0.0).astype(BF16)
        acts = mm_nt(hi, hid_ref[...]) + mm_nt(lo, hid_ref[...])
        acts_hi, acts_lo = split2(acts)
        hc_ref[0:256, :] = acts_hi
        hc_ref[256:512, :] = acts_lo

    acc = mm(hc_ref[...], g_ref[...])
    own_ref[...] = acc[0:64] + acc[256:320]
    r1_ref[...] = (acc[64:128] + acc[320:384]).astype(BF16)
    r2_ref[...] = (acc[128:192] + acc[384:448]).astype(BF16)
    r3_ref[...] = (acc[192:256] + acc[448:512]).astype(BF16)


def grad_part(me, hidden, tiled, out_grad):
    tokens, width = out_grad.shape
    steps = width // STEP
    return pl.pallas_call(
        grad_kernel,
        grid=(steps,),
        in_specs=[
            pl.BlockSpec(memory_space=pltpu.SMEM),
            whole((tokens, 256)),
            whole((512, 256)),
            pl.BlockSpec((tokens, STEP), lambda i: (0, i)),
        ],
        out_specs=[columns(64)] * 4,
        out_shape=[jax.ShapeDtypeStruct((64, width), d) for d in (F32, BF16, BF16, BF16)],
        scratch_shapes=[pltpu.VMEM((512, tokens), BF16)],
        compiler_params=PARAMS,
        name="grad_part",
    )(me, *hbm(hidden, tiled, out_grad))


def values_kernel(
    off0_ref, off1_ref, off2_ref, off3_ref, own_ref, r1_ref, r2_ref, r3_ref, mom_ref,
    expand_ref, gather_ref, look_ref, forward_ref, base_ref, own_look_ref, v0_ref, v1_ref,
    v2_ref, v3_ref, acc_ref,
):
    step = pl.program_id(0)
    steps = pl.num_programs(0)
    own = own_ref[...] + 0.9 * mm(forward_ref[...], packed(mom_ref[...]))
    base_ref[...] = own
    r1, r2, r3 = [ref[...].astype(F32) for ref in (r1_ref, r2_ref, r3_ref)]
    even = jnp.concatenate([x[0:32] for x in (own, r1, r2, r3)], axis=0)
    odd = jnp.concatenate([x[32:64] for x in (own, r1, r2, r3)], axis=0)
    off = jnp.concatenate(
        [off0_ref[...], off1_ref[...], off2_ref[...], off3_ref[...]], axis=0
    )
    target = mm(off, expand_ref[...])
    lane = (lax.broadcasted_iota(jnp.int32, target.shape, 1) & 63).astype(F32)
    upper = target >= 64.0
    place = jnp.where(upper, target - 64.0, target)
    mask = jnp.where(place == lane, 1.0, 0.0).astype(BF16)
    looked = []
    for t in range(STEP // 128):
        piece = mask[:, t * 128 : (t + 1) * 128]
        looked.append(mm(jnp.concatenate([piece, piece], axis=1), look_ref[...]))
    looked = jnp.concatenate(looked, axis=1)
    own_look_ref[0:32, :] = jnp.where(upper[0:32], 0.0, looked[0:32])
    own_look_ref[32:64, :] = jnp.where(upper[0:32], looked[0:32], 0.0)
    prod = jnp.where(upper, odd, even) * looked
    hi, lo = split2(prod)
    part = mm_nt(gather_ref[...], hi) + mm_nt(gather_ref[...], lo)

    @pl.when(step == 0)
    def _():
        acc_ref[...] = part

    @pl.when(step > 0)
    def _():
        acc_ref[...] += part

    @pl.when(step == steps - 1)
    def _():
        slot = lax.broadcasted_iota(jnp.int32, (32, 128), 1) >> 5
        for k, out in enumerate((v0_ref, v1_ref, v2_ref, v3_ref)):
            total = jnp.zeros((32, 128), F32)
            for x in range(4):
                rows = acc_ref[x * 32 : (x + 1) * 32, :]
                shift = ((x - k) * 32) % 128
                if shift:
                    rows = pltpu.roll(rows, shift, 1)
                total = jnp.where(slot == x, rows, total)
            out[...] = total


def values_part(offs, own, others, momentum, consts):
    width = own.shape[1]
    steps = width // STEP
    return pl.pallas_call(
        values_kernel,
        grid=(steps,),
        in_specs=[whole(offs[0].shape)] * 4
        + [columns(64)] * 5
        + [
            columns(consts["expand"].shape[0]),
            columns(consts["gather"].shape[0]),
            whole(consts["look"].shape),
            whole(consts["forward"].shape),
        ],
        out_specs=[columns(64)] * 2 + [whole((32, 128))] * 4,
        out_shape=[jax.ShapeDtypeStruct((64, width), F32)] * 2
        + [jax.ShapeDtypeStruct((32, 128), F32)] * 4,
        scratch_shapes=[pltpu.VMEM((128, 128), F32)],
        compiler_params=PARAMS,
        name="values_part",
    )(
        *offs, own, *others,
        *hbm(momentum, *(consts[k] for k in ("expand", "gather", "look", "forward"))),
    )


def join_kernel(v0_ref, v1_ref, v2_ref, v3_ref, vals_ref, sent_ref, *, sizes):
    n_y, n_z, n_c = sizes
    vals = v0_ref[...] + v1_ref[...] + v2_ref[...] + v3_ref[...]
    vals_ref[...] = vals
    for y in range(n_y):
        for c in range(n_c):
            at = (c * n_y + y) * 4
            for z in range(n_z):
                sent_ref[(y * n_z + z) * n_c + c] = vals[at : at + 4, :]


def join(parts, sizes):
    n_dp = sizes[0] * sizes[1] * sizes[2]
    return pl.pallas_call(
        functools.partial(join_kernel, sizes=sizes),
        out_shape=[jax.ShapeDtypeStruct((32, 128), F32), pltpu.VMEM((n_dp, 4, 128), F32)],
        name="join",
    )(*parts)


def total_kernel(
    me_ref, off_ref, val_ref, w_ref, wide_ref, wide_lo_ref, inverse_ref, ones_ref, out_ref, z_ref
):
    sources = off_ref.shape[0]
    width = w_ref.shape[1]
    count = width // 128
    index = lax.broadcasted_iota(jnp.int32, (128, 128), 0)
    for m in range(-(-count // 2)):
        acc = jnp.zeros((128, 128), F32)
        for r in range(sources):
            acc = acc + jnp.where(index == off_ref[r, m : m + 1, :], val_ref[r, m : m + 1, :], 0.0)
        hi, lo = split2(acc.T)
        mixed = mm(jnp.concatenate([hi, lo], axis=1), wide_ref[...]) + mm(hi, wide_lo_ref[...])
        for pair in range(2 * m, min(2 * m + 2, count)):
            at = (pair - 2 * m) * 64
            lanes = slice(pair * 128, (pair + 1) * 128)
            z_ref[0:32, lanes] = mixed[at : at + 32, 0:128] + mixed[at + 32 : at + 64, 256:384]
            z_ref[32:64, lanes] = mixed[at : at + 32, 128:256] + mixed[at + 32 : at + 64, 384:512]
    merged = mm(inverse_ref[...], packed(z_ref[...]))
    square = merged * merged
    part = square[0:8]
    for i in range(1, 8):
        part = part + square[i * 8 : (i + 1) * 8]
    part = jnp.concatenate([part[:, t * 128 : (t + 1) * 128] for t in range(count)], axis=0)
    hi, rest = split2(part)
    mid, low = split2(part - hi.astype(F32))
    ones = ones_ref[...]
    summed = mm(hi, ones) + mm(mid, ones) + mm(low, ones)
    me = me_ref[0]
    for t in range(count):
        lanes = slice(t * 128, (t + 1) * 128)
        mean = jnp.sum(summed[t * 8 : (t + 1) * 8], axis=0, keepdims=True) * (1.0 / 4096.0)
        update = jnp.tanh(merged[:, lanes] * lax.rsqrt(mean + 1e-06)).astype(BF16).astype(F32)
        stepped = (w_ref[:, lanes] - 0.05 * update).astype(BF16).astype(F32)
        for n in range(4):
            sent = jnp.where(me == n, update, stepped).astype(BF16)
            for y in range(4):
                out_ref[y * 4 + n, :, lanes] = sent


def total_part(me, off, vals, weights, consts):
    width = weights.shape[1]
    vmem = pl.BlockSpec(memory_space=pltpu.VMEM)
    return pl.pallas_call(
        total_kernel,
        in_specs=[pl.BlockSpec(memory_space=pltpu.SMEM)] + [vmem] * 7,
        out_specs=vmem,
        out_shape=pltpu.VMEM((16, 64, width), BF16),
        scratch_shapes=[pltpu.VMEM((64, width), F32)],
        compiler_params=PARAMS,
        name="total_part",
    )(
        me, off, vals, weights,
        *hbm(*(consts[k] for k in ("wide", "wide_lo", "inverse", "ones"))),
    )


def moment_kernel(
    base_ref, g1_ref, g2_ref, g3_ref, look_ref, vals_ref, gather_ref, inverse_ref, out_ref
):
    vals = vals_ref[...]
    slot = lax.broadcasted_iota(jnp.int32, (32, 128), 1) >> 5
    rows = [jnp.where(slot == x, vals, 0.0) for x in range(4)]
    tall = jnp.concatenate(rows, axis=0)
    fold = (
        (lax.broadcasted_iota(jnp.int32, (32, 128), 1) & 31)
        == lax.broadcasted_iota(jnp.int32, (32, 128), 0)
    )
    fold = jnp.where(fold, 1.0, 0.0).astype(BF16)
    hi, rest = split2(tall)
    mid, low = split2(tall - hi.astype(F32))
    gather = gather_ref[...]
    spread = jnp.zeros((32, out_ref.shape[1]), F32)
    for part in (hi, mid, low):
        spread = spread + mm(mm_nt(fold, part).astype(BF16), gather)
    left = base_ref[...]
    for ref in (g1_ref, g2_ref, g3_ref):
        left = left + ref[...].astype(F32)
    left = left - jnp.concatenate([spread, spread], axis=0) * look_ref[...]
    out_ref[...] = mm(inverse_ref[...], packed(left))


def moment_part(base, others, look, vals, consts):
    width = base.shape[1]
    return pl.pallas_call(
        moment_kernel,
        grid=(width // STEP,),
        in_specs=[columns(64)] * 5
        + [
            whole((32, 128)),
            columns(consts["gather"].shape[0]),
            whole(consts["inverse"].shape),
        ],
        out_specs=columns(64),
        out_shape=jax.ShapeDtypeStruct((64, width), F32),
        compiler_params=PARAMS,
        name="moment_part",
    )(base, *others, look, vals, *hbm(consts["gather"], consts["inverse"]))


def place_kernel(
    where_ref, got_ref, other_ref, w_ref, gathered_ref, update_ref, s_ref, u_ref, sem
):
    me = where_ref[0]
    size = got_ref.shape[2]
    copies = []

    def start(source, target):
        copies.append(pltpu.make_async_copy(source, target, sem.at[len(copies)]))
        copies[-1].start()

    for side, ref in enumerate((got_ref, other_ref)):
        core = where_ref[1] if side == 0 else 1 - where_ref[1]
        base = pl.multiple_of(core * (4 * size), 128)
        for y in range(4):
            for ahead in range(1, 4):
                node = (me + ahead) & 3
                row = pl.multiple_of(node * 64, 64)
                col = pl.multiple_of(base + y * size, 128)
                start(
                    ref.at[y * 4 + node], gathered_ref.at[pl.ds(row, 64), pl.ds(col, size)]
                )
    for side, ref in enumerate((got_ref, other_ref)):
        core = where_ref[1] if side == 0 else 1 - where_ref[1]
        base = pl.multiple_of(core * (4 * size), 128)
        for y in range(4):
            lanes = slice(y * size, (y + 1) * size)
            update = ref[y * 4 + me].astype(F32)
            u_ref[side, :, lanes] = update
            w = w_ref[:, pl.ds(pl.multiple_of(base + y * size, 128), size)]
            s_ref[side, :, lanes] = (w - 0.05 * update).astype(BF16)
        row = pl.multiple_of(me * 64, 64)
        start(s_ref.at[side], gathered_ref.at[pl.ds(row, 64), pl.ds(base, 4 * size)])
        start(u_ref.at[side], update_ref.at[:, pl.ds(base, 4 * size)])
    for copy in copies:
        copy.wait()


def place(where, got, other, weights):
    size = got.shape[2]
    anywhere = pl.BlockSpec(memory_space=pl.ANY)
    vmem = pl.BlockSpec(memory_space=pltpu.VMEM)
    return pl.pallas_call(
        place_kernel,
        in_specs=[pl.BlockSpec(memory_space=pltpu.SMEM), vmem, vmem, vmem],
        out_specs=[anywhere, anywhere],
        out_shape=[
            jax.ShapeDtypeStruct((256, 8 * size), BF16),
            jax.ShapeDtypeStruct((64, 8 * size), F32),
        ],
        scratch_shapes=[
            pltpu.VMEM((2, 64, 4 * size), BF16),
            pltpu.VMEM((2, 64, 4 * size), F32),
            pltpu.SemaphoreType.DMA((28,)),
        ],
        compiler_params=PARAMS,
        name="place",
    )(where, got, other, *hbm(weights))


def per_device(sizes, hidden, out_grad, momentum, positions, weights):
    n_y, n_z, n_c = sizes
    n_dp = n_y * n_z * n_c
    shares = n_y * n_c
    width = weights.shape[1]
    blocks = positions.shape[2]
    kept = positions.shape[3]
    size = width // shares
    per = blocks // shares
    consts = {k: jnp.asarray(v) for k, v in constants(blocks, shares).items()}
    me = lax.axis_index("node").astype(jnp.int32)
    y = lax.axis_index("y").astype(jnp.int32)
    core = lax.axis_index("c").astype(jnp.int32)
    replica = lax.axis_index(("y", "z", "c")).astype(jnp.int32)
    share = core * n_y + y
    mine = me[None]
    shift = lambda x, k: lax.ppermute(x, "node", [(i, (i + k) % 4) for i in range(4)])

    own_off = lax.dynamic_index_in_dim(positions[:, 0], replica, 0, keepdims=False)
    own_off = (own_off & 127).T.astype(BF16)
    offs = [own_off] + [shift(own_off, -k) for k in (1, 2, 3)]

    own, r1, r2, r3 = grad_part(mine, hidden, consts["tiled"], out_grad)
    base, look, v0, v1, v2, v3 = values_part(offs, own, (r1, r2, r3), momentum[0], consts)
    vals, sent = join([v0, shift(v1, 1), shift(v2, 2), shift(v3, 3)], sizes)

    positions, weights_later, v0 = lax.optimization_barrier((positions, weights, v0))
    share_off = lax.dynamic_slice_in_dim(positions[:, 0], share * per, per, axis=1) & 127
    share_off = share_off.reshape(n_dp, per * kept)
    share_off = jnp.pad(share_off, ((0, 0), (0, 512 - per * kept)), constant_values=-1)
    share_off = share_off.reshape(n_dp, 4, 128)
    share_weights = lax.dynamic_slice_in_dim(weights_later, share * size, size, axis=1)
    sent, share_off, share_weights, r1, r2, r3 = lax.optimization_barrier(
        (sent, share_off, share_weights, r1, r2, r3)
    )
    g1, g2, g3 = shift(r1, 1), shift(r2, 2), shift(r3, 3)

    every = lax.all_to_all(sent, ("y", "z", "c"), 0, 0, tiled=True)
    every, g1, g3 = lax.optimization_barrier((every, g1, g3))
    sent = total_part(mine, share_off, every, share_weights, consts)
    sent, g2 = lax.optimization_barrier((sent, g2))
    got = lax.all_to_all(sent, ("y", "node"), 0, 0, tiled=True)
    got, vals = lax.optimization_barrier((got, vals))
    other = lax.ppermute(got, "c", [(0, 1), (1, 0)])
    new_moment = moment_part(base, (g1, g2, g3), look, vals, consts)
    gathered, update = place(jnp.stack([me, core]), got, other, weights)
    return (new_moment[None], update, gathered)


def solution(mesh):
    n_dp = mesh.shape["dp"]
    sizes = (4, n_dp // 8, 2)
    parts = Mesh(mesh.devices.reshape(*sizes, mesh.shape["node"]), ("y", "z", "c", "node"))
    dp = ("y", "z", "c")
    return jax.shard_map(
        functools.partial(per_device, sizes),
        mesh=parts,
        in_specs=(
            P(dp + ("node",), None),
            P(dp + ("node",), None),
            P(dp, "node", None),
            P(None, "node", None, None),
            P("node", None),
        ),
        out_specs=(P(dp, "node", None), P("node", None), P()),
        check_vma=False,
    )
```

```python
import functools

import jax
import jax.numpy as jnp
import ml_dtypes
import numpy as np
from jax import lax
from jax.experimental import pallas as pl
from jax.experimental.pallas import tpu as pltpu
from jax.sharding import Mesh
from jax.sharding import PartitionSpec as P

F32 = jnp.float32
BF16 = jnp.bfloat16
VMEM_LIMIT = 32 * 1024 * 1024


def split_np(x):
    hi = x.astype(ml_dtypes.bfloat16)
    lo = (x - hi.astype(np.float64)).astype(ml_dtypes.bfloat16)
    return hi, lo


def basis(size):
    freq = np.arange(size, dtype=np.float64)[:, None]
    place = np.arange(size, dtype=np.float64)[None, :]
    table = np.cos(np.pi * (2.0 * place + 1.0) * freq / (2.0 * size)) * np.sqrt(2.0 / size)
    return np.where(freq == 0, table * np.sqrt(0.5), table)


def constants(blocks, shares):
    table = basis(64)
    order = np.concatenate([np.arange(0, 64, 2), np.arange(1, 64, 2)])
    hi, lo = split_np(table[order])
    tiled = np.concatenate([np.tile(hi, (4, 4)), np.tile(lo, (4, 4))]).astype(np.float32)
    forward = np.concatenate([hi, hi, lo], axis=1)
    inverse = np.concatenate([hi.T, hi.T, lo.T], axis=1)
    look = np.concatenate(split_np(np.kron(np.eye(2), table)), axis=0)
    spread = np.zeros((2, 64, 2, 2, 2, 64))
    for p in range(2):
        for t in range(2):
            spread[t, :, p, t, p, :] = table
    wide_hi, wide_lo = split_np(spread.reshape(128, 512))
    wide = np.concatenate([wide_hi, wide_hi], axis=0)
    ones = np.kron(np.eye(2), np.ones((64, 64))).astype(ml_dtypes.bfloat16)
    expand = np.kron(np.eye(blocks), np.ones((1, 64))).astype(ml_dtypes.bfloat16)
    per = blocks // shares
    gather = np.zeros((4, shares, 4, blocks * 64), ml_dtypes.bfloat16)
    for b in range(blocks):
        q, x = divmod(b % per, 4)
        gather[x, b // per, q, b * 64 : (b + 1) * 64] = 1
    gather = gather.reshape(16 * shares, blocks * 64)
    return dict(
        tiled=tiled, forward=forward, inverse=inverse, look=look, wide=wide, wide_lo=wide_lo,
        ones=ones, expand=expand, gather=gather,
    )


def split2(x):
    hi = x.astype(BF16)
    return hi, (x - hi.astype(F32)).astype(BF16)


def mm(a, b):
    return jnp.dot(a, b, preferred_element_type=F32)


def mm_nt(a, b):
    return lax.dot_general(a, b, (((1,), (1,)), ((), ())), preferred_element_type=F32)


def packed(x):
    hi, lo = split2(x)
    return jnp.concatenate([hi, lo, hi], axis=0)


def hbm(*arrays):
    return [pltpu.with_memory_space_constraint(x, pltpu.HBM) for x in arrays]


def vmem(*arrays):
    return [pltpu.with_memory_space_constraint(x, pltpu.VMEM) for x in arrays]


PARAMS = pltpu.CompilerParams(vmem_limit_bytes=VMEM_LIMIT)
STEP = 2560


def whole(shape):
    return pl.BlockSpec(shape, lambda i: (0,) * len(shape))


def columns(rows):
    return pl.BlockSpec((rows, STEP), lambda i: (0, i))


def grad_kernel(
    me_ref, hid_ref, tiled_ref, g_ref, own_ref, r1_ref, r2_ref, r3_ref, hc_ref
):
    step = pl.program_id(0)

    @pl.when(step == 0)
    def _():
        me = me_ref[0]
        row = lax.broadcasted_iota(jnp.int32, (256, 256), 0) >> 6
        col = lax.broadcasted_iota(jnp.int32, (256, 256), 1) >> 6
        keep = ((col - row - me + 8) & 3) == 0
        hi = jnp.where(keep, tiled_ref[0:256, :], 0.0).astype(BF16)
        lo = jnp.where(keep, tiled_ref[256:512, :], 0.0).astype(BF16)
        acts = mm_nt(hi, hid_ref[...]) + mm_nt(lo, hid_ref[...])
        acts_hi, acts_lo = split2(acts)
        hc_ref[0:256, :] = acts_hi
        hc_ref[256:512, :] = acts_lo

    acc = mm(hc_ref[...], g_ref[...])
    own_ref[...] = acc[0:64] + acc[256:320]
    r1_ref[...] = (acc[64:128] + acc[320:384]).astype(BF16)
    r2_ref[...] = (acc[128:192] + acc[384:448]).astype(BF16)
    r3_ref[...] = (acc[192:256] + acc[448:512]).astype(BF16)


def grad_part(me, hidden, tiled, out_grad):
    tokens, width = out_grad.shape
    steps = width // STEP
    return pl.pallas_call(
        grad_kernel,
        grid=(steps,),
        in_specs=[
            pl.BlockSpec(memory_space=pltpu.SMEM),
            whole((tokens, 256)),
            whole((512, 256)),
            pl.BlockSpec((tokens, STEP), lambda i: (0, i)),
        ],
        out_specs=[columns(64)] * 4,
        out_shape=[jax.ShapeDtypeStruct((64, width), d) for d in (F32, BF16, BF16, BF16)],
        scratch_shapes=[pltpu.VMEM((512, tokens), BF16)],
        compiler_params=PARAMS,
        name="grad_part",
    )(me, *hbm(hidden, tiled, out_grad))


def values_kernel(
    off0_ref, off1_ref, off2_ref, off3_ref, own_ref, r1_ref, r2_ref, r3_ref, mom_ref,
    expand_ref, gather_ref, look_ref, forward_ref, base_ref, own_look_ref, v0_ref, v1_ref,
    v2_ref, v3_ref, acc_ref,
):
    step = pl.program_id(0)
    steps = pl.num_programs(0)
    own = own_ref[...] + 0.9 * mm(forward_ref[...], packed(mom_ref[...]))
    base_ref[...] = own
    r1, r2, r3 = [ref[...].astype(F32) for ref in (r1_ref, r2_ref, r3_ref)]
    even = jnp.concatenate([x[0:32] for x in (own, r1, r2, r3)], axis=0)
    odd = jnp.concatenate([x[32:64] for x in (own, r1, r2, r3)], axis=0)
    off = jnp.concatenate(
        [off0_ref[...], off1_ref[...], off2_ref[...], off3_ref[...]], axis=0
    )
    target = mm(off, expand_ref[...])
    lane = (lax.broadcasted_iota(jnp.int32, target.shape, 1) & 63).astype(F32)
    upper = target >= 64.0
    place = jnp.where(upper, target - 64.0, target)
    mask = jnp.where(place == lane, 1.0, 0.0).astype(BF16)
    count = STEP // 128
    stack = jnp.concatenate([mask[:, t * 128 : (t + 1) * 128] for t in range(count)], axis=0)
    looked = mm(jnp.concatenate([stack, stack], axis=1), look_ref[...])
    looked = jnp.concatenate([looked[t * 128 : (t + 1) * 128] for t in range(count)], axis=1)
    own_look_ref[0:32, :] = jnp.where(upper[0:32], 0.0, looked[0:32])
    own_look_ref[32:64, :] = jnp.where(upper[0:32], looked[0:32], 0.0)
    prod = jnp.where(upper, odd, even) * looked
    hi, lo = split2(prod)
    part = mm_nt(gather_ref[...], hi) + mm_nt(gather_ref[...], lo)

    @pl.when(step == 0)
    def _():
        acc_ref[...] = part

    @pl.when(step > 0)
    def _():
        acc_ref[...] += part

    @pl.when(step == steps - 1)
    def _():
        slot = lax.broadcasted_iota(jnp.int32, (32, 128), 1) >> 5
        for k, out in enumerate((v0_ref, v1_ref, v2_ref, v3_ref)):
            total = jnp.zeros((32, 128), F32)
            for x in range(4):
                rows = acc_ref[x * 32 : (x + 1) * 32, :]
                shift = ((x - k) * 32) % 128
                if shift:
                    rows = pltpu.roll(rows, shift, 1)
                total = jnp.where(slot == x, rows, total)
            out[...] = total


def values_part(offs, own, others, momentum, consts):
    width = own.shape[1]
    steps = width // STEP
    return pl.pallas_call(
        values_kernel,
        grid=(steps,),
        in_specs=[whole(offs[0].shape)] * 4
        + [columns(64)] * 5
        + [
            columns(consts["expand"].shape[0]),
            columns(consts["gather"].shape[0]),
            whole(consts["look"].shape),
            whole(consts["forward"].shape),
        ],
        out_specs=[columns(64)] * 2 + [whole((32, 128))] * 4,
        out_shape=[jax.ShapeDtypeStruct((64, width), F32)] * 2
        + [pltpu.VMEM((32, 128), F32)] * 4,
        scratch_shapes=[pltpu.VMEM((128, 128), F32)],
        compiler_params=PARAMS,
        name="values_part",
    )(
        *offs, own, *others,
        *hbm(momentum, *(consts[k] for k in ("expand", "gather", "look", "forward"))),
    )


def join_kernel(v0_ref, v1_ref, v2_ref, v3_ref, vals_ref, sent_ref, *, sizes):
    n_y, n_z, n_c = sizes
    vals = v0_ref[...] + v1_ref[...] + v2_ref[...] + v3_ref[...]
    vals_ref[...] = vals
    for y in range(n_y):
        for c in range(n_c):
            at = (c * n_y + y) * 4
            for z in range(n_z):
                sent_ref[(y * n_z + z) * n_c + c] = vals[at : at + 4, :]


def join(parts, sizes):
    n_dp = sizes[0] * sizes[1] * sizes[2]
    return pl.pallas_call(
        functools.partial(join_kernel, sizes=sizes),
        out_shape=[jax.ShapeDtypeStruct((32, 128), F32), pltpu.VMEM((n_dp, 4, 128), F32)],
        name="join",
    )(*vmem(*parts))


def total_kernel(
    me_ref, off_ref, val_ref, w_ref, wide_hbm, wide_lo_hbm, inverse_hbm, ones_hbm, out_ref,
    z_ref, wide_ref, wide_lo_ref, inverse_ref, ones_ref, sem,
):
    tables = (
        (wide_hbm, wide_ref), (wide_lo_hbm, wide_lo_ref), (inverse_hbm, inverse_ref),
        (ones_hbm, ones_ref),
    )
    copies = [pltpu.make_async_copy(a, b, sem.at[k]) for k, (a, b) in enumerate(tables)]
    for copy in copies:
        copy.start()
    sources = off_ref.shape[0]
    width = w_ref.shape[1]
    count = width // 128
    index = lax.broadcasted_iota(jnp.int32, (128, 128), 0)
    for m in range(-(-count // 2)):
        acc = jnp.zeros((128, 128), F32)
        for r in range(sources):
            acc = acc + jnp.where(index == off_ref[r, m : m + 1, :], val_ref[r, m : m + 1, :], 0.0)
        if m == 0:
            for copy in copies:
                copy.wait()
        hi, lo = split2(acc.T)
        mixed = mm(jnp.concatenate([hi, lo], axis=1), wide_ref[...]) + mm(hi, wide_lo_ref[...])
        for pair in range(2 * m, min(2 * m + 2, count)):
            at = (pair - 2 * m) * 64
            lanes = slice(pair * 128, (pair + 1) * 128)
            z_ref[0:32, lanes] = mixed[at : at + 32, 0:128] + mixed[at + 32 : at + 64, 256:384]
            z_ref[32:64, lanes] = mixed[at : at + 32, 128:256] + mixed[at + 32 : at + 64, 384:512]
    merged = mm(inverse_ref[...], packed(z_ref[...]))
    square = merged * merged
    part = square[0:8]
    for i in range(1, 8):
        part = part + square[i * 8 : (i + 1) * 8]
    part = jnp.concatenate([part[:, t * 128 : (t + 1) * 128] for t in range(count)], axis=0)
    hi, rest = split2(part)
    mid, low = split2(part - hi.astype(F32))
    ones = ones_ref[...]
    summed = mm(hi, ones) + mm(mid, ones) + mm(low, ones)
    me = me_ref[0]
    for t in range(count):
        lanes = slice(t * 128, (t + 1) * 128)
        mean = jnp.sum(summed[t * 8 : (t + 1) * 8], axis=0, keepdims=True) * (1.0 / 4096.0)
        update = jnp.tanh(merged[:, lanes] * lax.rsqrt(mean + 1e-06)).astype(BF16).astype(F32)
        stepped = (w_ref[:, lanes] - 0.05 * update).astype(BF16).astype(F32)
        for n in range(4):
            sent = jnp.where(me == n, update, stepped).astype(BF16)
            for y in range(4):
                out_ref[y * 4 + n, :, lanes] = sent


def total_part(me, off, vals, weights, consts):
    width = weights.shape[1]
    here = pl.BlockSpec(memory_space=pltpu.VMEM)
    anywhere = pl.BlockSpec(memory_space=pl.ANY)
    tables = [consts[k] for k in ("wide", "wide_lo", "inverse", "ones")]
    return pl.pallas_call(
        total_kernel,
        in_specs=[pl.BlockSpec(memory_space=pltpu.SMEM)] + [here] * 3 + [anywhere] * 4,
        out_specs=here,
        out_shape=pltpu.VMEM((16, 64, width), BF16),
        scratch_shapes=[pltpu.VMEM((64, width), F32)]
        + [pltpu.VMEM(x.shape, x.dtype) for x in tables]
        + [pltpu.SemaphoreType.DMA((4,))],
        compiler_params=PARAMS,
        name="total_part",
    )(me, *vmem(off, vals, weights), *hbm(*tables))


def moment_kernel(
    base_ref, g1_ref, g2_ref, g3_ref, look_ref, vals_ref, gather_ref, inverse_ref, out_ref
):
    vals = vals_ref[...]
    slot = lax.broadcasted_iota(jnp.int32, (32, 128), 1) >> 5
    rows = [jnp.where(slot == x, vals, 0.0) for x in range(4)]
    tall = jnp.concatenate(rows, axis=0)
    fold = (
        (lax.broadcasted_iota(jnp.int32, (32, 128), 1) & 31)
        == lax.broadcasted_iota(jnp.int32, (32, 128), 0)
    )
    fold = jnp.where(fold, 1.0, 0.0).astype(BF16)
    hi, rest = split2(tall)
    mid, low = split2(tall - hi.astype(F32))
    gather = gather_ref[...]
    spread = jnp.zeros((32, out_ref.shape[1]), F32)
    for part in (hi, mid, low):
        spread = spread + mm(mm_nt(fold, part).astype(BF16), gather)
    left = base_ref[...]
    for ref in (g1_ref, g2_ref, g3_ref):
        left = left + ref[...].astype(F32)
    left = left - jnp.concatenate([spread, spread], axis=0) * look_ref[...]
    out_ref[...] = mm(inverse_ref[...], packed(left))


def moment_part(base, others, look, vals, consts):
    width = base.shape[1]
    return pl.pallas_call(
        moment_kernel,
        grid=(width // STEP,),
        in_specs=[columns(64)] * 5
        + [
            whole((32, 128)),
            columns(consts["gather"].shape[0]),
            whole(consts["inverse"].shape),
        ],
        out_specs=columns(64),
        out_shape=jax.ShapeDtypeStruct((64, width), F32),
        compiler_params=PARAMS,
        name="moment_part",
    )(base, *others, look, vals, *hbm(consts["gather"], consts["inverse"]))


def place_kernel(where_ref, got_ref, w_ref, *refs):
    gathered_ref, update_ref, s_ref, u_ref, sem = refs[-5:]
    me = where_ref[0]
    size = got_ref.shape[2]
    base = pl.multiple_of(where_ref[1] * (4 * size), 128)
    copies = []

    def start(source, target):
        copies.append(pltpu.make_async_copy(source, target, sem.at[len(copies)]))
        copies[-1].start()

    for y in range(4):
        for ahead in range(1, 4):
            node = (me + ahead) & 3
            row = pl.multiple_of(node * 64, 64)
            col = pl.multiple_of(base + y * size, 128)
            start(got_ref.at[y * 4 + node], gathered_ref.at[pl.ds(row, 64), pl.ds(col, size)])
    for y in range(4):
        lanes = slice(y * size, (y + 1) * size)
        update = got_ref[y * 4 + me].astype(F32)
        u_ref[:, lanes] = update
        w = w_ref[:, pl.ds(pl.multiple_of(base + y * size, 128), size)]
        s_ref[:, lanes] = (w - 0.05 * update).astype(BF16)
    row = pl.multiple_of(me * 64, 64)
    start(s_ref, gathered_ref.at[pl.ds(row, 64), pl.ds(base, 4 * size)])
    start(u_ref, update_ref.at[:, pl.ds(base, 4 * size)])
    for copy in copies:
        copy.wait()


def place(where, got, weights, before):
    size = got.shape[2]
    anywhere = pl.BlockSpec(memory_space=pl.ANY)
    here = pl.BlockSpec(memory_space=pltpu.VMEM)
    return pl.pallas_call(
        place_kernel,
        in_specs=[pl.BlockSpec(memory_space=pltpu.SMEM), here, here] + [anywhere] * len(before),
        out_specs=[anywhere, anywhere],
        out_shape=[pltpu.HBM((256, 8 * size), BF16), pltpu.HBM((64, 8 * size), F32)],
        input_output_aliases={3 + i: i for i in range(len(before))},
        scratch_shapes=[
            pltpu.VMEM((64, 4 * size), BF16),
            pltpu.VMEM((64, 4 * size), F32),
            pltpu.SemaphoreType.DMA((14,)),
        ],
        compiler_params=PARAMS,
        name="place",
    )(where, *vmem(got), *hbm(weights, *before))


def per_device(sizes, hidden, out_grad, momentum, positions, weights):
    n_y, n_z, n_c = sizes
    n_dp = n_y * n_z * n_c
    shares = n_y * n_c
    width = weights.shape[1]
    blocks = positions.shape[2]
    kept = positions.shape[3]
    size = width // shares
    per = blocks // shares
    consts = {k: jnp.asarray(v) for k, v in constants(blocks, shares).items()}
    me = lax.axis_index("node").astype(jnp.int32)
    y = lax.axis_index("y").astype(jnp.int32)
    core = lax.axis_index("c").astype(jnp.int32)
    replica = lax.axis_index(("y", "z", "c")).astype(jnp.int32)
    share = core * n_y + y
    mine = me[None]
    shift = lambda x, k: lax.ppermute(x, "node", [(i, (i + k) % 4) for i in range(4)])

    own_off = lax.dynamic_index_in_dim(positions[:, 0], replica, 0, keepdims=False)
    own_off = (own_off & 127).T.astype(BF16)
    offs = [own_off] + [shift(own_off, -k) for k in (1, 2, 3)]

    own, r1, r2, r3 = grad_part(mine, hidden, consts["tiled"], out_grad)
    base, look, v0, v1, v2, v3 = values_part(offs, own, (r1, r2, r3), momentum[0], consts)
    v1, v2, v3 = shift(v1, 1), shift(v2, 2), shift(v3, 3)
    v1, v2, v3, r1, r2, r3 = lax.optimization_barrier((v1, v2, v3, r1, r2, r3))
    g1, g2, g3 = shift(r1, 1), shift(r2, 2), shift(r3, 3)
    vals, sent = join([v0, v1, v2, v3], sizes)
    share, sent = lax.optimization_barrier((share, sent))

    share_off = lax.dynamic_slice_in_dim(positions[:, 0], share * per, per, axis=1) & 127
    share_off = share_off.reshape(n_dp, per * kept)
    share_off = jnp.pad(share_off, ((0, 0), (0, 512 - per * kept)), constant_values=-1)
    share_off = share_off.reshape(n_dp, 4, 128)
    share_weights = lax.dynamic_slice_in_dim(weights, share * size, size, axis=1)
    every = lax.all_to_all(sent, ("y", "z", "c"), 0, 0, tiled=True)
    sent = total_part(mine, share_off, every, share_weights, consts)
    sent, g1, g2, g3 = lax.optimization_barrier((sent, g1, g2, g3))
    got = lax.all_to_all(sent, ("y", "node"), 0, 0, tiled=True)
    new_moment = moment_part(base, (g1, g2, g3), look, vals, consts)
    got, new_moment = lax.optimization_barrier((got, new_moment))
    other = lax.ppermute(got, "c", [(0, 1), (1, 0)])
    done = place(jnp.stack([me, core]), got, weights, [])
    gathered, update = place(jnp.stack([me, 1 - core]), other, weights, done)
    return (new_moment[None], update, gathered)


def solution(mesh):
    n_dp = mesh.shape["dp"]
    sizes = (4, n_dp // 8, 2)
    parts = Mesh(mesh.devices.reshape(*sizes, mesh.shape["node"]), ("y", "z", "c", "node"))
    dp = ("y", "z", "c")
    return jax.shard_map(
        functools.partial(per_device, sizes),
        mesh=parts,
        in_specs=(
            P(dp + ("node",), None),
            P(dp + ("node",), None),
            P(dp, "node", None),
            P(None, "node", None, None),
            P("node", None),
        ),
        out_specs=(P(dp, "node", None), P("node", None), P()),
        check_vma=False,
    )
```

```python
import functools

import jax
import jax.numpy as jnp
import ml_dtypes
import numpy as np
from jax import lax
from jax.experimental import pallas as pl
from jax.experimental.pallas import tpu as pltpu
from jax.sharding import Mesh
from jax.sharding import PartitionSpec as P

F32 = jnp.float32
BF16 = jnp.bfloat16
VMEM_LIMIT = 32 * 1024 * 1024


def split_np(x):
    hi = x.astype(ml_dtypes.bfloat16)
    lo = (x - hi.astype(np.float64)).astype(ml_dtypes.bfloat16)
    return hi, lo


def basis(size):
    freq = np.arange(size, dtype=np.float64)[:, None]
    place = np.arange(size, dtype=np.float64)[None, :]
    table = np.cos(np.pi * (2.0 * place + 1.0) * freq / (2.0 * size)) * np.sqrt(2.0 / size)
    return np.where(freq == 0, table * np.sqrt(0.5), table)


def constants(blocks, shares):
    table = basis(64)
    order = np.concatenate([np.arange(0, 64, 2), np.arange(1, 64, 2)])
    hi, lo = split_np(table[order])
    tiled = np.concatenate([np.tile(hi, (4, 4)), np.tile(lo, (4, 4))]).astype(np.float32)
    forward = np.concatenate([hi, hi, lo], axis=1)
    inverse = np.concatenate([hi.T, hi.T, lo.T], axis=1)
    look = np.concatenate(split_np(np.kron(np.eye(2), table)), axis=0)
    spread = np.zeros((2, 64, 2, 2, 2, 64))
    for p in range(2):
        for t in range(2):
            spread[t, :, p, t, p, :] = table
    wide_hi, wide_lo = split_np(spread.reshape(128, 512))
    wide = np.concatenate([wide_hi, wide_hi], axis=0)
    ones = np.kron(np.eye(2), np.ones((64, 64))).astype(ml_dtypes.bfloat16)
    expand = np.kron(np.eye(blocks), np.ones((1, 64))).astype(ml_dtypes.bfloat16)
    per = blocks // shares
    gather = np.zeros((4, shares, 4, blocks * 64), ml_dtypes.bfloat16)
    for b in range(blocks):
        q, x = divmod(b % per, 4)
        gather[x, b // per, q, b * 64 : (b + 1) * 64] = 1
    gather = gather.reshape(16 * shares, blocks * 64)
    return dict(
        tiled=tiled, forward=forward, inverse=inverse, look=look, wide=wide, wide_lo=wide_lo,
        ones=ones, expand=expand, gather=gather,
    )


def split2(x):
    hi = x.astype(BF16)
    return hi, (x - hi.astype(F32)).astype(BF16)


def mm(a, b):
    return jnp.dot(a, b, preferred_element_type=F32)


def mm_nt(a, b):
    return lax.dot_general(a, b, (((1,), (1,)), ((), ())), preferred_element_type=F32)


def packed(x):
    hi, lo = split2(x)
    return jnp.concatenate([hi, lo, hi], axis=0)


def hbm(*arrays):
    return [pltpu.with_memory_space_constraint(x, pltpu.HBM) for x in arrays]


def vmem(*arrays):
    return [pltpu.with_memory_space_constraint(x, pltpu.VMEM) for x in arrays]


PARAMS = pltpu.CompilerParams(vmem_limit_bytes=VMEM_LIMIT)
STEP = 2560


def whole(shape):
    return pl.BlockSpec(shape, lambda i: (0,) * len(shape))


def columns(rows):
    return pl.BlockSpec((rows, STEP), lambda i: (0, i))


def grad_kernel(
    me_ref, hid_ref, tiled_ref, g_ref, own_ref, r1_ref, r2_ref, r3_ref, hc_ref
):
    step = pl.program_id(0)

    @pl.when(step == 0)
    def _():
        me = me_ref[0]
        row = lax.broadcasted_iota(jnp.int32, (256, 256), 0) >> 6
        col = lax.broadcasted_iota(jnp.int32, (256, 256), 1) >> 6
        keep = ((col - row - me + 8) & 3) == 0
        hi = jnp.where(keep, tiled_ref[0:256, :], 0.0).astype(BF16)
        lo = jnp.where(keep, tiled_ref[256:512, :], 0.0).astype(BF16)
        acts = mm_nt(hi, hid_ref[...]) + mm_nt(lo, hid_ref[...])
        hc_ref[...] = acts.astype(BF16)

    acc = mm(hc_ref[...], g_ref[...])
    own_ref[...] = acc[0:64]
    r1_ref[...] = acc[64:128].astype(BF16)
    r2_ref[...] = acc[128:192].astype(BF16)
    r3_ref[...] = acc[192:256].astype(BF16)


def grad_part(me, hidden, tiled, out_grad):
    tokens, width = out_grad.shape
    steps = width // STEP
    return pl.pallas_call(
        grad_kernel,
        grid=(steps,),
        in_specs=[
            pl.BlockSpec(memory_space=pltpu.SMEM),
            whole((tokens, 256)),
            whole((512, 256)),
            pl.BlockSpec((tokens, STEP), lambda i: (0, i)),
        ],
        out_specs=[columns(64)] * 4,
        out_shape=[jax.ShapeDtypeStruct((64, width), d) for d in (F32, BF16, BF16, BF16)],
        scratch_shapes=[pltpu.VMEM((256, tokens), BF16)],
        compiler_params=PARAMS,
        name="grad_part",
    )(me, *hbm(hidden, tiled, out_grad))


def values_kernel(
    off0_ref, off1_ref, off2_ref, off3_ref, own_ref, r1_ref, r2_ref, r3_ref, mom_ref,
    expand_ref, gather_ref, look_ref, forward_ref, base_ref, own_look_ref, v0_ref, v1_ref,
    v2_ref, v3_ref, acc_ref,
):
    step = pl.program_id(0)
    steps = pl.num_programs(0)
    own = own_ref[...] + 0.9 * mm(forward_ref[...], packed(mom_ref[...]))
    base_ref[...] = own
    r1, r2, r3 = [ref[...].astype(F32) for ref in (r1_ref, r2_ref, r3_ref)]
    even = jnp.concatenate([x[0:32] for x in (own, r1, r2, r3)], axis=0)
    odd = jnp.concatenate([x[32:64] for x in (own, r1, r2, r3)], axis=0)
    off = jnp.concatenate(
        [off0_ref[...], off1_ref[...], off2_ref[...], off3_ref[...]], axis=0
    )
    target = mm(off, expand_ref[...])
    lane = (lax.broadcasted_iota(jnp.int32, target.shape, 1) & 63).astype(F32)
    upper = target >= 64.0
    place = jnp.where(upper, target - 64.0, target)
    mask = jnp.where(place == lane, 1.0, 0.0).astype(BF16)
    count = STEP // 128
    stack = jnp.concatenate([mask[:, t * 128 : (t + 1) * 128] for t in range(count)], axis=0)
    looked = mm(jnp.concatenate([stack, stack], axis=1), look_ref[...])
    looked = jnp.concatenate([looked[t * 128 : (t + 1) * 128] for t in range(count)], axis=1)
    own_look_ref[0:32, :] = jnp.where(upper[0:32], 0.0, looked[0:32])
    own_look_ref[32:64, :] = jnp.where(upper[0:32], looked[0:32], 0.0)
    prod = jnp.where(upper, odd, even) * looked
    hi, lo = split2(prod)
    part = mm_nt(gather_ref[...], hi) + mm_nt(gather_ref[...], lo)

    @pl.when(step == 0)
    def _():
        acc_ref[...] = part

    @pl.when(step > 0)
    def _():
        acc_ref[...] += part

    @pl.when(step == steps - 1)
    def _():
        slot = lax.broadcasted_iota(jnp.int32, (32, 128), 1) >> 5
        for k, out in enumerate((v0_ref, v1_ref, v2_ref, v3_ref)):
            total = jnp.zeros((32, 128), F32)
            for x in range(4):
                rows = acc_ref[x * 32 : (x + 1) * 32, :]
                shift = ((x - k) * 32) % 128
                if shift:
                    rows = pltpu.roll(rows, shift, 1)
                total = jnp.where(slot == x, rows, total)
            out[...] = total


def values_part(offs, own, others, momentum, consts):
    width = own.shape[1]
    steps = width // STEP
    return pl.pallas_call(
        values_kernel,
        grid=(steps,),
        in_specs=[whole(offs[0].shape)] * 4
        + [columns(64)] * 5
        + [
            columns(consts["expand"].shape[0]),
            columns(consts["gather"].shape[0]),
            whole(consts["look"].shape),
            whole(consts["forward"].shape),
        ],
        out_specs=[columns(64)] * 2 + [whole((32, 128))] * 4,
        out_shape=[pltpu.HBM((64, width), F32)] * 2
        + [pltpu.VMEM((32, 128), F32)] * 4,
        scratch_shapes=[pltpu.VMEM((128, 128), F32)],
        compiler_params=PARAMS,
        name="values_part",
    )(
        *offs, own, *others,
        *hbm(momentum, *(consts[k] for k in ("expand", "gather", "look", "forward"))),
    )


def join_kernel(v0_ref, v1_ref, v2_ref, v3_ref, vals_ref, sent_ref, *, sizes):
    n_y, n_z, n_c = sizes
    vals = v0_ref[...] + v1_ref[...] + v2_ref[...] + v3_ref[...]
    vals_ref[...] = vals
    for y in range(n_y):
        for c in range(n_c):
            at = (c * n_y + y) * 4
            for z in range(n_z):
                sent_ref[(y * n_z + z) * n_c + c] = vals[at : at + 4, :]


def join(parts, sizes):
    n_dp = sizes[0] * sizes[1] * sizes[2]
    return pl.pallas_call(
        functools.partial(join_kernel, sizes=sizes),
        out_shape=[jax.ShapeDtypeStruct((32, 128), F32), pltpu.VMEM((n_dp, 4, 128), F32)],
        name="join",
    )(*vmem(*parts))


def total_kernel(
    me_ref, off_ref, val_ref, w_ref, wide_hbm, wide_lo_hbm, inverse_hbm, ones_hbm, out_ref,
    z_ref, wide_ref, wide_lo_ref, inverse_ref, ones_ref, sem,
):
    tables = (
        (wide_hbm, wide_ref), (wide_lo_hbm, wide_lo_ref), (inverse_hbm, inverse_ref),
        (ones_hbm, ones_ref),
    )
    copies = [pltpu.make_async_copy(a, b, sem.at[k]) for k, (a, b) in enumerate(tables)]
    for copy in copies:
        copy.start()
    sources = off_ref.shape[0]
    width = w_ref.shape[1]
    count = width // 128
    index = lax.broadcasted_iota(jnp.int32, (128, 128), 0)
    for m in range(-(-count // 2)):
        acc = jnp.zeros((128, 128), F32)
        for r in range(sources):
            acc = acc + jnp.where(index == off_ref[r, m : m + 1, :], val_ref[r, m : m + 1, :], 0.0)
        if m == 0:
            for copy in copies:
                copy.wait()
        hi, lo = split2(acc.T)
        mixed = mm(jnp.concatenate([hi, lo], axis=1), wide_ref[...]) + mm(hi, wide_lo_ref[...])
        for pair in range(2 * m, min(2 * m + 2, count)):
            at = (pair - 2 * m) * 64
            lanes = slice(pair * 128, (pair + 1) * 128)
            z_ref[0:32, lanes] = mixed[at : at + 32, 0:128] + mixed[at + 32 : at + 64, 256:384]
            z_ref[32:64, lanes] = mixed[at : at + 32, 128:256] + mixed[at + 32 : at + 64, 384:512]
    merged = mm(inverse_ref[...], packed(z_ref[...]))
    square = merged * merged
    part = square[0:8]
    for i in range(1, 8):
        part = part + square[i * 8 : (i + 1) * 8]
    part = jnp.concatenate([part[:, t * 128 : (t + 1) * 128] for t in range(count)], axis=0)
    hi, rest = split2(part)
    mid, low = split2(part - hi.astype(F32))
    ones = ones_ref[...]
    summed = mm(hi, ones) + mm(mid, ones) + mm(low, ones)
    me = me_ref[0]
    for t in range(count):
        lanes = slice(t * 128, (t + 1) * 128)
        mean = jnp.sum(summed[t * 8 : (t + 1) * 8], axis=0, keepdims=True) * (1.0 / 4096.0)
        update = jnp.tanh(merged[:, lanes] * lax.rsqrt(mean + 1e-06)).astype(BF16).astype(F32)
        stepped = (w_ref[:, lanes] - 0.05 * update).astype(BF16).astype(F32)
        for n in range(4):
            sent = jnp.where(me == n, update, stepped).astype(BF16)
            for y in range(4):
                out_ref[y * 4 + n, :, lanes] = sent


def total_part(me, off, vals, weights, consts):
    width = weights.shape[1]
    here = pl.BlockSpec(memory_space=pltpu.VMEM)
    anywhere = pl.BlockSpec(memory_space=pl.ANY)
    tables = [consts[k] for k in ("wide", "wide_lo", "inverse", "ones")]
    return pl.pallas_call(
        total_kernel,
        in_specs=[pl.BlockSpec(memory_space=pltpu.SMEM)] + [here] * 3 + [anywhere] * 4,
        out_specs=here,
        out_shape=pltpu.VMEM((16, 64, width), BF16),
        scratch_shapes=[pltpu.VMEM((64, width), F32)]
        + [pltpu.VMEM(x.shape, x.dtype) for x in tables]
        + [pltpu.SemaphoreType.DMA((4,))],
        compiler_params=PARAMS,
        name="total_part",
    )(me, *vmem(off, vals, weights), *hbm(*tables))


def moment_kernel(
    base_ref, g1_ref, g2_ref, g3_ref, look_ref, vals_ref, gather_ref, inverse_ref, out_ref
):
    vals = vals_ref[...]
    slot = lax.broadcasted_iota(jnp.int32, (32, 128), 1) >> 5
    rows = [jnp.where(slot == x, vals, 0.0) for x in range(4)]
    tall = jnp.concatenate(rows, axis=0)
    fold = (
        (lax.broadcasted_iota(jnp.int32, (32, 128), 1) & 31)
        == lax.broadcasted_iota(jnp.int32, (32, 128), 0)
    )
    fold = jnp.where(fold, 1.0, 0.0).astype(BF16)
    hi, rest = split2(tall)
    mid, low = split2(tall - hi.astype(F32))
    gather = gather_ref[...]
    spread = jnp.zeros((32, out_ref.shape[1]), F32)
    for part in (hi, mid, low):
        spread = spread + mm(mm_nt(fold, part).astype(BF16), gather)
    left = base_ref[...]
    for ref in (g1_ref, g2_ref, g3_ref):
        left = left + ref[...].astype(F32)
    left = left - jnp.concatenate([spread, spread], axis=0) * look_ref[...]
    out_ref[...] = mm(inverse_ref[...], packed(left))


def moment_part(base, others, look, vals, consts):
    width = base.shape[1]
    return pl.pallas_call(
        moment_kernel,
        grid=(width // STEP,),
        in_specs=[columns(64)] * 5
        + [
            whole((32, 128)),
            columns(consts["gather"].shape[0]),
            whole(consts["inverse"].shape),
        ],
        out_specs=columns(64),
        out_shape=jax.ShapeDtypeStruct((64, width), F32),
        compiler_params=PARAMS,
        name="moment_part",
    )(
        *hbm(base), *others, *hbm(look), vals, *hbm(consts["gather"], consts["inverse"])
    )


def place_kernel(where_ref, got_ref, w_ref, *refs):
    gathered_ref, update_ref, s_ref, u_ref, sem = refs[-5:]
    me = where_ref[0]
    size = got_ref.shape[2]
    base = pl.multiple_of(where_ref[1] * (4 * size), 128)
    copies = []

    def start(source, target):
        copies.append(pltpu.make_async_copy(source, target, sem.at[len(copies)]))
        copies[-1].start()

    for y in range(4):
        for ahead in range(1, 4):
            node = (me + ahead) & 3
            row = pl.multiple_of(node * 64, 64)
            col = pl.multiple_of(base + y * size, 128)
            start(got_ref.at[y * 4 + node], gathered_ref.at[pl.ds(row, 64), pl.ds(col, size)])
    for y in range(4):
        lanes = slice(y * size, (y + 1) * size)
        update = got_ref[y * 4 + me].astype(F32)
        u_ref[:, lanes] = update
        w = w_ref[:, pl.ds(pl.multiple_of(base + y * size, 128), size)]
        s_ref[:, lanes] = (w - 0.05 * update).astype(BF16)
    row = pl.multiple_of(me * 64, 64)
    start(s_ref, gathered_ref.at[pl.ds(row, 64), pl.ds(base, 4 * size)])
    start(u_ref, update_ref.at[:, pl.ds(base, 4 * size)])
    for copy in copies:
        copy.wait()


def place(where, got, weights, before):
    size = got.shape[2]
    anywhere = pl.BlockSpec(memory_space=pl.ANY)
    here = pl.BlockSpec(memory_space=pltpu.VMEM)
    return pl.pallas_call(
        place_kernel,
        in_specs=[pl.BlockSpec(memory_space=pltpu.SMEM), here, here] + [anywhere] * len(before),
        out_specs=[anywhere, anywhere],
        out_shape=[pltpu.HBM((256, 8 * size), BF16), pltpu.HBM((64, 8 * size), F32)],
        input_output_aliases={3 + i: i for i in range(len(before))},
        scratch_shapes=[
            pltpu.VMEM((64, 4 * size), BF16),
            pltpu.VMEM((64, 4 * size), F32),
            pltpu.SemaphoreType.DMA((14,)),
        ],
        compiler_params=PARAMS,
        name="place",
    )(where, *vmem(got), *hbm(weights, *before))


def per_device(sizes, hidden, out_grad, momentum, positions, weights):
    n_y, n_z, n_c = sizes
    n_dp = n_y * n_z * n_c
    shares = n_y * n_c
    width = weights.shape[1]
    blocks = positions.shape[2]
    kept = positions.shape[3]
    size = width // shares
    per = blocks // shares
    consts = {k: jnp.asarray(v) for k, v in constants(blocks, shares).items()}
    me = lax.axis_index("node").astype(jnp.int32)
    y = lax.axis_index("y").astype(jnp.int32)
    core = lax.axis_index("c").astype(jnp.int32)
    replica = lax.axis_index(("y", "z", "c")).astype(jnp.int32)
    share = core * n_y + y
    mine = me[None]
    shift = lambda x, k: lax.ppermute(x, "node", [(i, (i + k) % 4) for i in range(4)])

    own_off = lax.dynamic_index_in_dim(positions[:, 0], replica, 0, keepdims=False)
    own_off = (own_off & 127).T.astype(BF16)
    offs = [own_off] + [shift(own_off, -k) for k in (1, 2, 3)]

    own, r1, r2, r3 = grad_part(mine, hidden, consts["tiled"], out_grad)
    base, look, v0, v1, v2, v3 = values_part(offs, own, (r1, r2, r3), momentum[0], consts)
    v1, v2, v3 = shift(v1, 1), shift(v2, 2), shift(v3, 3)
    v1, v2, v3, r1, r2, r3 = lax.optimization_barrier((v1, v2, v3, r1, r2, r3))
    g1, g2, g3 = shift(r1, 1), shift(r2, 2), shift(r3, 3)
    vals, sent = join([v0, v1, v2, v3], sizes)
    share, sent = lax.optimization_barrier((share, sent))

    share_off = lax.dynamic_slice_in_dim(positions[:, 0], share * per, per, axis=1) & 127
    share_off = share_off.reshape(n_dp, per * kept)
    share_off = jnp.pad(share_off, ((0, 0), (0, 512 - per * kept)), constant_values=-1)
    share_off = share_off.reshape(n_dp, 4, 128)
    share_weights = lax.dynamic_slice_in_dim(weights, share * size, size, axis=1)
    every = lax.all_to_all(sent, ("y", "z", "c"), 0, 0, tiled=True)
    sent = total_part(mine, share_off, every, share_weights, consts)
    sent, g1, g2, g3 = lax.optimization_barrier((sent, g1, g2, g3))
    got = lax.all_to_all(sent, ("y", "node"), 0, 0, tiled=True)
    new_moment = moment_part(base, (g1, g2, g3), look, vals, consts)
    got, new_moment = lax.optimization_barrier((got, new_moment))
    other = lax.ppermute(got, "c", [(0, 1), (1, 0)])
    done = place(jnp.stack([me, core]), got, weights, [])
    gathered, update = place(jnp.stack([me, 1 - core]), other, weights, done)
    return (new_moment[None], update, gathered)


def solution(mesh):
    n_dp = mesh.shape["dp"]
    sizes = (4, n_dp // 8, 2)
    parts = Mesh(mesh.devices.reshape(*sizes, mesh.shape["node"]), ("y", "z", "c", "node"))
    dp = ("y", "z", "c")
    return jax.shard_map(
        functools.partial(per_device, sizes),
        mesh=parts,
        in_specs=(
            P(dp + ("node",), None),
            P(dp + ("node",), None),
            P(dp, "node", None),
            P(None, "node", None, None),
            P("node", None),
        ),
        out_specs=(P(dp, "node", None), P("node", None), P()),
        check_vma=False,
    )
```

```python
import functools

import jax
import jax.numpy as jnp
import ml_dtypes
import numpy as np
from jax import lax
from jax.experimental import pallas as pl
from jax.experimental.pallas import tpu as pltpu
from jax.sharding import Mesh
from jax.sharding import PartitionSpec as P

F32 = jnp.float32
BF16 = jnp.bfloat16
VMEM_LIMIT = 32 * 1024 * 1024


def split_np(x):
    hi = x.astype(ml_dtypes.bfloat16)
    lo = (x - hi.astype(np.float64)).astype(ml_dtypes.bfloat16)
    return hi, lo


def basis(size):
    freq = np.arange(size, dtype=np.float64)[:, None]
    place = np.arange(size, dtype=np.float64)[None, :]
    table = np.cos(np.pi * (2.0 * place + 1.0) * freq / (2.0 * size)) * np.sqrt(2.0 / size)
    return np.where(freq == 0, table * np.sqrt(0.5), table)


def constants(blocks, shares):
    table = basis(64)
    order = np.concatenate([np.arange(0, 64, 2), np.arange(1, 64, 2)])
    hi, lo = split_np(table[order])
    tiled = np.concatenate([np.tile(hi, (4, 4)), np.tile(lo, (4, 4))]).astype(np.float32)
    forward = np.concatenate([hi, hi, lo], axis=1)
    inverse = np.concatenate([hi.T, hi.T, lo.T], axis=1)
    look = np.concatenate(split_np(np.kron(np.eye(2), table)), axis=0)
    spread = np.zeros((2, 64, 2, 2, 2, 64))
    for p in range(2):
        for t in range(2):
            spread[t, :, p, t, p, :] = table
    wide_hi, wide_lo = split_np(spread.reshape(128, 512))
    wide = np.concatenate([wide_hi, wide_hi], axis=0)
    ones = np.kron(np.eye(2), np.ones((64, 64))).astype(ml_dtypes.bfloat16)
    expand = np.kron(np.eye(blocks), np.ones((1, 64))).astype(ml_dtypes.bfloat16)
    per = blocks // shares
    gather = np.zeros((4, shares, 4, blocks * 64), ml_dtypes.bfloat16)
    for b in range(blocks):
        q, x = divmod(b % per, 4)
        gather[x, b // per, q, b * 64 : (b + 1) * 64] = 1
    gather = gather.reshape(16 * shares, blocks * 64)
    return dict(
        tiled=tiled, forward=forward, inverse=inverse, look=look, wide=wide, wide_lo=wide_lo,
        ones=ones, expand=expand, gather=gather,
    )


def split2(x):
    hi = x.astype(BF16)
    return hi, (x - hi.astype(F32)).astype(BF16)


def mm(a, b):
    return jnp.dot(a, b, preferred_element_type=F32)


def mm_nt(a, b):
    return lax.dot_general(a, b, (((1,), (1,)), ((), ())), preferred_element_type=F32)


def packed(x):
    hi, lo = split2(x)
    return jnp.concatenate([hi, lo, hi], axis=0)


def hbm(*arrays):
    return [pltpu.with_memory_space_constraint(x, pltpu.HBM) for x in arrays]


def vmem(*arrays):
    return [pltpu.with_memory_space_constraint(x, pltpu.VMEM) for x in arrays]


PARAMS = pltpu.CompilerParams(vmem_limit_bytes=VMEM_LIMIT)
STEP = 2560


def whole(shape):
    return pl.BlockSpec(shape, lambda i: (0,) * len(shape))


def columns(rows):
    return pl.BlockSpec((rows, STEP), lambda i: (0, i))


def grad_kernel(
    me_ref, hid_ref, tiled_ref, g_ref, own_ref, a1_ref, a2_ref, a3_ref, b1_ref, b2_ref, b3_ref,
    hc_ref,
):
    step = pl.program_id(0)

    @pl.when(step == 0)
    def _():
        me = me_ref[0]
        row = lax.broadcasted_iota(jnp.int32, (256, 256), 0) >> 6
        col = lax.broadcasted_iota(jnp.int32, (256, 256), 1) >> 6
        keep = ((col - row - me + 8) & 3) == 0
        hi = jnp.where(keep, tiled_ref[0:256, :], 0.0).astype(BF16)
        lo = jnp.where(keep, tiled_ref[256:512, :], 0.0).astype(BF16)
        acts = mm_nt(hi, hid_ref[...]) + mm_nt(lo, hid_ref[...])
        hc_ref[...] = acts.astype(BF16)

    acc = mm(hc_ref[...], g_ref[...])
    own_ref[...] = acc[0:64]
    step = pl.program_id(0)
    for half, refs in enumerate(((a1_ref, a2_ref, a3_ref), (b1_ref, b2_ref, b3_ref))):

        @pl.when(step == half)
        def _(refs=refs):
            for k, ref in enumerate(refs):
                ref[...] = acc[64 * (k + 1) : 64 * (k + 2)].astype(BF16)


def grad_part(me, hidden, tiled, out_grad):
    tokens, width = out_grad.shape
    steps = width // STEP
    return pl.pallas_call(
        grad_kernel,
        grid=(steps,),
        in_specs=[
            pl.BlockSpec(memory_space=pltpu.SMEM),
            whole((tokens, 256)),
            whole((512, 256)),
            pl.BlockSpec((tokens, STEP), lambda i: (0, i)),
        ],
        out_specs=[columns(64)] + [whole((64, STEP))] * 6,
        out_shape=[jax.ShapeDtypeStruct((64, width), F32)]
        + [jax.ShapeDtypeStruct((64, STEP), BF16)] * 6,
        scratch_shapes=[pltpu.VMEM((256, tokens), BF16)],
        compiler_params=PARAMS,
        name="grad_part",
    )(me, *hbm(hidden, tiled, out_grad))


def values_kernel(
    off0_ref, off1_ref, off2_ref, off3_ref, own_ref, a1_ref, a2_ref, a3_ref, b1_ref, b2_ref,
    b3_ref, mom_ref,
    expand_ref, gather_ref, look_ref, forward_ref, base_ref, own_look_ref, v0_ref, v1_ref,
    v2_ref, v3_ref, acc_ref,
):
    step = pl.program_id(0)
    steps = pl.num_programs(0)
    own = own_ref[...] + 0.9 * mm(forward_ref[...], packed(mom_ref[...]))
    base_ref[...] = own
    r1, r2, r3 = [
        jnp.where(step == 0, a[...].astype(F32), b[...].astype(F32))
        for a, b in ((a1_ref, b1_ref), (a2_ref, b2_ref), (a3_ref, b3_ref))
    ]
    even = jnp.concatenate([x[0:32] for x in (own, r1, r2, r3)], axis=0)
    odd = jnp.concatenate([x[32:64] for x in (own, r1, r2, r3)], axis=0)
    off = jnp.concatenate(
        [off0_ref[...], off1_ref[...], off2_ref[...], off3_ref[...]], axis=0
    )
    target = mm(off, expand_ref[...])
    lane = (lax.broadcasted_iota(jnp.int32, target.shape, 1) & 63).astype(F32)
    upper = target >= 64.0
    place = jnp.where(upper, target - 64.0, target)
    mask = jnp.where(place == lane, 1.0, 0.0).astype(BF16)
    count = STEP // 128
    stack = jnp.concatenate([mask[:, t * 128 : (t + 1) * 128] for t in range(count)], axis=0)
    looked = mm(jnp.concatenate([stack, stack], axis=1), look_ref[...])
    looked = jnp.concatenate([looked[t * 128 : (t + 1) * 128] for t in range(count)], axis=1)
    own_look_ref[0:32, :] = jnp.where(upper[0:32], 0.0, looked[0:32])
    own_look_ref[32:64, :] = jnp.where(upper[0:32], looked[0:32], 0.0)
    prod = jnp.where(upper, odd, even) * looked
    hi, lo = split2(prod)
    part = mm_nt(gather_ref[...], hi) + mm_nt(gather_ref[...], lo)

    @pl.when(step == 0)
    def _():
        acc_ref[...] = part

    @pl.when(step > 0)
    def _():
        acc_ref[...] += part

    @pl.when(step == steps - 1)
    def _():
        slot = lax.broadcasted_iota(jnp.int32, (32, 128), 1) >> 5
        for k, out in enumerate((v0_ref, v1_ref, v2_ref, v3_ref)):
            total = jnp.zeros((32, 128), F32)
            for x in range(4):
                rows = acc_ref[x * 32 : (x + 1) * 32, :]
                shift = ((x - k) * 32) % 128
                if shift:
                    rows = pltpu.roll(rows, shift, 1)
                total = jnp.where(slot == x, rows, total)
            out[...] = total


def values_part(offs, own, others, momentum, consts):
    width = own.shape[1]
    steps = width // STEP
    return pl.pallas_call(
        values_kernel,
        grid=(steps,),
        in_specs=[whole(offs[0].shape)] * 4
        + [columns(64)]
        + [whole((64, STEP))] * 6
        + [columns(64)]
        + [
            columns(consts["expand"].shape[0]),
            columns(consts["gather"].shape[0]),
            whole(consts["look"].shape),
            whole(consts["forward"].shape),
        ],
        out_specs=[columns(64)] * 2 + [whole((32, 128))] * 4,
        out_shape=[pltpu.HBM((64, width), F32)] * 2
        + [pltpu.VMEM((32, 128), F32)] * 4,
        scratch_shapes=[pltpu.VMEM((128, 128), F32)],
        compiler_params=PARAMS,
        name="values_part",
    )(
        *offs, own, *others,
        *hbm(momentum, *(consts[k] for k in ("expand", "gather", "look", "forward"))),
    )


def join_kernel(v0_ref, v1_ref, v2_ref, v3_ref, vals_ref, sent_ref, *, sizes):
    n_y, n_z, n_c = sizes
    vals = v0_ref[...] + v1_ref[...] + v2_ref[...] + v3_ref[...]
    vals_ref[...] = vals
    for y in range(n_y):
        for c in range(n_c):
            at = (c * n_y + y) * 4
            for z in range(n_z):
                sent_ref[(y * n_z + z) * n_c + c] = vals[at : at + 4, :]


def join(parts, sizes):
    n_dp = sizes[0] * sizes[1] * sizes[2]
    return pl.pallas_call(
        functools.partial(join_kernel, sizes=sizes),
        out_shape=[jax.ShapeDtypeStruct((32, 128), F32), pltpu.VMEM((n_dp, 4, 128), F32)],
        name="join",
    )(*vmem(*parts))


def total_kernel(
    me_ref, off_ref, val_ref, w_ref, wide_hbm, wide_lo_hbm, inverse_hbm, ones_hbm, out_ref,
    z_ref, wide_ref, wide_lo_ref, inverse_ref, ones_ref, sem,
):
    tables = (
        (wide_hbm, wide_ref), (wide_lo_hbm, wide_lo_ref), (inverse_hbm, inverse_ref),
        (ones_hbm, ones_ref),
    )
    copies = [pltpu.make_async_copy(a, b, sem.at[k]) for k, (a, b) in enumerate(tables)]
    for copy in copies:
        copy.start()
    sources = off_ref.shape[0]
    width = w_ref.shape[1]
    count = width // 128
    index = lax.broadcasted_iota(jnp.int32, (128, 128), 0)
    for m in range(-(-count // 2)):
        acc = jnp.zeros((128, 128), F32)
        for r in range(sources):
            acc = acc + jnp.where(index == off_ref[r, m : m + 1, :], val_ref[r, m : m + 1, :], 0.0)
        if m == 0:
            for copy in copies:
                copy.wait()
        hi, lo = split2(acc.T)
        mixed = mm(jnp.concatenate([hi, lo], axis=1), wide_ref[...]) + mm(hi, wide_lo_ref[...])
        for pair in range(2 * m, min(2 * m + 2, count)):
            at = (pair - 2 * m) * 64
            lanes = slice(pair * 128, (pair + 1) * 128)
            z_ref[0:32, lanes] = mixed[at : at + 32, 0:128] + mixed[at + 32 : at + 64, 256:384]
            z_ref[32:64, lanes] = mixed[at : at + 32, 128:256] + mixed[at + 32 : at + 64, 384:512]
    merged = mm(inverse_ref[...], packed(z_ref[...]))
    square = merged * merged
    part = square[0:8]
    for i in range(1, 8):
        part = part + square[i * 8 : (i + 1) * 8]
    part = jnp.concatenate([part[:, t * 128 : (t + 1) * 128] for t in range(count)], axis=0)
    hi, rest = split2(part)
    mid, low = split2(part - hi.astype(F32))
    ones = ones_ref[...]
    summed = mm(hi, ones) + mm(mid, ones) + mm(low, ones)
    me = me_ref[0]
    for t in range(count):
        lanes = slice(t * 128, (t + 1) * 128)
        mean = jnp.sum(summed[t * 8 : (t + 1) * 8], axis=0, keepdims=True) * (1.0 / 4096.0)
        update = jnp.tanh(merged[:, lanes] * lax.rsqrt(mean + 1e-06)).astype(BF16).astype(F32)
        stepped = (w_ref[:, lanes] - 0.05 * update).astype(BF16).astype(F32)
        for n in range(4):
            sent = jnp.where(me == n, update, stepped).astype(BF16)
            for y in range(4):
                out_ref[y * 4 + n, :, lanes] = sent


def total_part(me, off, vals, weights, consts):
    width = weights.shape[1]
    here = pl.BlockSpec(memory_space=pltpu.VMEM)
    anywhere = pl.BlockSpec(memory_space=pl.ANY)
    tables = [consts[k] for k in ("wide", "wide_lo", "inverse", "ones")]
    return pl.pallas_call(
        total_kernel,
        in_specs=[pl.BlockSpec(memory_space=pltpu.SMEM)] + [here] * 3 + [anywhere] * 4,
        out_specs=here,
        out_shape=pltpu.VMEM((16, 64, width), BF16),
        scratch_shapes=[pltpu.VMEM((64, width), F32)]
        + [pltpu.VMEM(x.shape, x.dtype) for x in tables]
        + [pltpu.SemaphoreType.DMA((4,))],
        compiler_params=PARAMS,
        name="total_part",
    )(me, *vmem(off, vals, weights), *hbm(*tables))


def moment_kernel(
    base_ref, near_a_ref, far_a_ref, near_b_ref, far_b_ref, look_ref, vals_ref, gather_ref, inverse_ref, out_ref
):
    vals = vals_ref[...]
    slot = lax.broadcasted_iota(jnp.int32, (32, 128), 1) >> 5
    rows = [jnp.where(slot == x, vals, 0.0) for x in range(4)]
    tall = jnp.concatenate(rows, axis=0)
    fold = (
        (lax.broadcasted_iota(jnp.int32, (32, 128), 1) & 31)
        == lax.broadcasted_iota(jnp.int32, (32, 128), 0)
    )
    fold = jnp.where(fold, 1.0, 0.0).astype(BF16)
    hi, rest = split2(tall)
    mid, low = split2(tall - hi.astype(F32))
    gather = gather_ref[...]
    spread = jnp.zeros((32, out_ref.shape[1]), F32)
    for part in (hi, mid, low):
        spread = spread + mm(mm_nt(fold, part).astype(BF16), gather)
    sum_a = near_a_ref[...].astype(F32) + far_a_ref[...].astype(F32)
    sum_b = near_b_ref[...].astype(F32) + far_b_ref[...].astype(F32)
    left = base_ref[...] + jnp.where(pl.program_id(0) == 0, sum_a, sum_b)
    left = left - jnp.concatenate([spread, spread], axis=0) * look_ref[...]
    out_ref[...] = mm(inverse_ref[...], packed(left))


def moment_part(base, others, look, vals, consts):
    width = base.shape[1]
    return pl.pallas_call(
        moment_kernel,
        grid=(width // STEP,),
        in_specs=[columns(64)]
        + [whole((64, STEP))] * 4
        + [columns(64)]
        + [
            whole((32, 128)),
            columns(consts["gather"].shape[0]),
            whole(consts["inverse"].shape),
        ],
        out_specs=columns(64),
        out_shape=jax.ShapeDtypeStruct((64, width), F32),
        compiler_params=PARAMS,
        name="moment_part",
    )(
        *hbm(base), *others, *hbm(look), vals, *hbm(consts["gather"], consts["inverse"])
    )


def place_kernel(where_ref, got_ref, w_ref, *refs):
    gathered_ref, update_ref, s_ref, u_ref, sem = refs[-5:]
    me = where_ref[0]
    size = got_ref.shape[2]
    base = pl.multiple_of(where_ref[1] * (4 * size), 128)
    copies = []

    def start(source, target):
        copies.append(pltpu.make_async_copy(source, target, sem.at[len(copies)]))
        copies[-1].start()

    for y in range(4):
        for ahead in range(1, 4):
            node = (me + ahead) & 3
            row = pl.multiple_of(node * 64, 64)
            col = pl.multiple_of(base + y * size, 128)
            start(got_ref.at[y * 4 + node], gathered_ref.at[pl.ds(row, 64), pl.ds(col, size)])
    for y in range(4):
        lanes = slice(y * size, (y + 1) * size)
        update = got_ref[y * 4 + me].astype(F32)
        u_ref[:, lanes] = update
        w = w_ref[:, pl.ds(pl.multiple_of(base + y * size, 128), size)]
        s_ref[:, lanes] = (w - 0.05 * update).astype(BF16)
    row = pl.multiple_of(me * 64, 64)
    start(s_ref, gathered_ref.at[pl.ds(row, 64), pl.ds(base, 4 * size)])
    start(u_ref, update_ref.at[:, pl.ds(base, 4 * size)])
    for copy in copies:
        copy.wait()


def place(where, got, weights, before):
    size = got.shape[2]
    anywhere = pl.BlockSpec(memory_space=pl.ANY)
    here = pl.BlockSpec(memory_space=pltpu.VMEM)
    return pl.pallas_call(
        place_kernel,
        in_specs=[pl.BlockSpec(memory_space=pltpu.SMEM), here, here] + [anywhere] * len(before),
        out_specs=[anywhere, anywhere],
        out_shape=[pltpu.HBM((256, 8 * size), BF16), pltpu.HBM((64, 8 * size), F32)],
        input_output_aliases={3 + i: i for i in range(len(before))},
        scratch_shapes=[
            pltpu.VMEM((64, 4 * size), BF16),
            pltpu.VMEM((64, 4 * size), F32),
            pltpu.SemaphoreType.DMA((14,)),
        ],
        compiler_params=PARAMS,
        name="place",
    )(where, *vmem(got), *hbm(weights, *before))


def per_device(sizes, hidden, out_grad, momentum, positions, weights):
    n_y, n_z, n_c = sizes
    n_dp = n_y * n_z * n_c
    shares = n_y * n_c
    width = weights.shape[1]
    blocks = positions.shape[2]
    kept = positions.shape[3]
    size = width // shares
    per = blocks // shares
    consts = {k: jnp.asarray(v) for k, v in constants(blocks, shares).items()}
    me = lax.axis_index("node").astype(jnp.int32)
    y = lax.axis_index("y").astype(jnp.int32)
    core = lax.axis_index("c").astype(jnp.int32)
    replica = lax.axis_index(("y", "z", "c")).astype(jnp.int32)
    share = core * n_y + y
    mine = me[None]
    shift = lambda x, k: lax.ppermute(x, "node", [(i, (i + k) % 4) for i in range(4)])

    own_off = lax.dynamic_index_in_dim(positions[:, 0], replica, 0, keepdims=False)
    own_off = (own_off & 127).T.astype(BF16)
    offs = [own_off] + [shift(own_off, -k) for k in (1, 2, 3)]

    own, *others = grad_part(mine, hidden, consts["tiled"], out_grad)
    base, look, v0, v1, v2, v3 = values_part(offs, own, others, momentum[0], consts)
    v1, v2, v3 = shift(v1, 1), shift(v2, 2), shift(v3, 3)
    v1, v2, v3, others = lax.optimization_barrier((v1, v2, v3, others))
    a1, a2, a3, b1, b2, b3 = others
    relay_a, relay_b = shift(a2, 1), shift(b2, -1)
    near_b, near_a = shift(b1, 1), shift(a3, -1)
    vals, sent = join([v0, v1, v2, v3], sizes)
    share, sent = lax.optimization_barrier((share, sent))

    share_off = lax.dynamic_slice_in_dim(positions[:, 0], share * per, per, axis=1) & 127
    share_off = share_off.reshape(n_dp, per * kept)
    share_off = jnp.pad(share_off, ((0, 0), (0, 512 - per * kept)), constant_values=-1)
    share_off = share_off.reshape(n_dp, 4, 128)
    share_weights = lax.dynamic_slice_in_dim(weights, share * size, size, axis=1)
    every = lax.all_to_all(sent, ("y", "z", "c"), 0, 0, tiled=True)
    relay_a, relay_b, near_a, near_b = lax.optimization_barrier(
        (relay_a, relay_b, near_a, near_b)
    )
    far_a = shift(relay_a + a1, 1)
    far_b = shift(relay_b + b3, -1)
    sent = total_part(mine, share_off, every, share_weights, consts)
    sent, near_a, near_b, far_a, far_b = lax.optimization_barrier(
        (sent, near_a, near_b, far_a, far_b)
    )
    got = lax.all_to_all(sent, ("y", "node"), 0, 0, tiled=True)
    new_moment = moment_part(base, (near_a, far_a, near_b, far_b), look, vals, consts)
    got, new_moment = lax.optimization_barrier((got, new_moment))
    other = lax.ppermute(got, "c", [(0, 1), (1, 0)])
    done = place(jnp.stack([me, core]), got, weights, [])
    gathered, update = place(jnp.stack([me, 1 - core]), other, weights, done)
    return (new_moment[None], update, gathered)


def solution(mesh):
    n_dp = mesh.shape["dp"]
    sizes = (4, n_dp // 8, 2)
    parts = Mesh(mesh.devices.reshape(*sizes, mesh.shape["node"]), ("y", "z", "c", "node"))
    dp = ("y", "z", "c")
    return jax.shard_map(
        functools.partial(per_device, sizes),
        mesh=parts,
        in_specs=(
            P(dp + ("node",), None),
            P(dp + ("node",), None),
            P(dp, "node", None),
            P(None, "node", None, None),
            P("node", None),
        ),
        out_specs=(P(dp, "node", None), P("node", None), P()),
        check_vma=False,
    )
```
